128 devices in a mesh: enc: 4 (over z), region: 32 (over y, x, core).
Axes of the slice: x: 4, y: 4, z: 4, core: 2. Of those that a mesh axis runs over, the one named last changes fastest.
Arguments:
- embeddings: bfloat16 [131072, 1536], P(('enc', 'region')), may hold values from -6 to 6
- tile_position: int32 [131072], P(('enc', 'region')), may hold values from 0 to 131071, as said below
- w_in: bfloat16 [1536, 768], replicated, may hold values from -0.15625 to 0.15625
- ln_gain: bfloat16 [768], replicated, may hold values from 0.099609375 to 1.8984375
- w_query: bfloat16 [768, 768], replicated, may hold values from -0.14505926 to 0.14505926
- w_key: bfloat16 [768, 768], replicated, may hold values from -1.8222618 to 1.8222618
- w_value: bfloat16 [768, 768], replicated, may hold values from -0.21875 to 0.21875
- w_out: bfloat16 [768, 768], replicated, may hold values from -0.21875 to 0.21875
- near_lengths: int32 [4, 256], replicated, may hold values from 1 to 256, 32768 in all within a row
- far_lengths: int32 [4, 64], replicated, may hold values from 1 to 1024, 32768 in all within a row
- tissue: int32 [131072], P(('enc', 'region')), may hold values 0 or 1
- hospital: int32 [4], replicated, may hold values from 0 to 1, as said below
- w_kernel: float32 [768, 256], replicated, may hold values from -0.21875 to 0.21875
Outputs:
- features: bfloat16 [131072, 768], P(('enc', 'region'))
- statistic: float32 [], replicated
- kernel_grad: float32 [768, 256], replicated
The draws below stay inside these ranges and needn't reach their ends.
Inputs may be any that keep to these rules, and one draw needn't show every extreme that they name: `tile_position`: every number of 0 to 131071 appears once; the 1024 rows of each device hold exactly 8 positions of each device's block of 1024 consecutive tile positions. `hospital`: each of the two labels is held by at least one of the 4 slides.
All inputs are finite; a program needn't handle non-finite values. No bound on the sum of `tissue` on one device may be relied on, other than what follows from the above.
Results may differ from the reference program's by a relative error of at most 0.012.
Values may be sent and summed in bfloat16 or wider, within the bound.
A program may use at most 128 MiB of HBM per device.

```python
import math
import jax
import jax.numpy as jnp
import numpy as np
from jax import lax

DIN = 1536
D = 768
HEADS = 16
P_SIZE = 256
REGION = 256
DILATION = 4
ROWS = 1024
SENDERS = 128
CAP = 8
SLIDES = 4
SLIDE_LEN = 32768
TILES = 131072
NEAR_SPAN = 256
NSEG_NEAR = 256
NSEG_FAR = 64
REG_DEV = 4
NREG = 512
N_REGION = 32


def draw_tile_position(key, part):
    slot_keys = jax.random.split(jax.random.fold_in(key, 11), SENDERS)
    slot_order = jax.vmap(lambda one_key: jax.random.permutation(one_key, ROWS))(slot_keys).astype(jnp.int32)
    owners = jnp.arange(SENDERS, dtype=jnp.int32)[:, None] * ROWS + slot_order
    by_sender = owners.reshape(SENDERS, SENDERS, CAP).transpose(1, 0, 2).reshape(SENDERS, ROWS)
    shuffle_keys = jax.random.split(jax.random.fold_in(key, 12), SENDERS)
    shuffles = jax.vmap(lambda one_key: jax.random.permutation(one_key, ROWS))(shuffle_keys).astype(jnp.int32)
    mixed = jnp.take_along_axis(by_sender, shuffles, axis=1)
    return mixed.reshape(SENDERS * ROWS).astype(jnp.int32)


def query_key_pair(key):
    first = jax.random.normal(jax.random.fold_in(key, 101), (D, D), jnp.float32)
    second = jax.random.normal(jax.random.fold_in(key, 102), (D, D), jnp.float32)
    first = jnp.clip(first, -4.0, 4.0) * D ** (-0.5)
    second = jnp.clip(second, -4.0, 4.0) * D ** (-0.5)
    return (first, second)


def draw_w_query(key, part):
    first, second = query_key_pair(key)
    return first.astype(jnp.bfloat16)


def draw_w_key(key, part):
    first, second = query_key_pair(key)
    return second.astype(jnp.bfloat16)


def draw_hospital(key, part):
    order = jax.random.permutation(jax.random.fold_in(key, 21), SLIDES).astype(jnp.int32)
    split = jax.random.randint(jax.random.fold_in(key, 22), (), 1, SLIDES, dtype=jnp.int32)
    return (order < split).astype(jnp.int32)


def plant(drawn, stream_key, low, largest):
    place = [jax.random.randint(jax.random.fold_in(stream_key, axis), (), 0, length) for axis, length in enumerate(drawn.shape)]
    main_axis = drawn.shape.index(max(drawn.shape))
    beside = place[:main_axis] + [(place[main_axis] + 1) % drawn.shape[main_axis]] + place[main_axis + 1:]
    return drawn.at[tuple(place)].set(low).at[tuple(beside)].set(largest)


def block_levels(key, dims, cuts, low, high):
    loudness = 1.0
    for axis_at, shards_of in cuts:
        draws = jax.random.uniform(jax.random.fold_in(jax.random.fold_in(key, 6), axis_at), (shards_of,), jnp.float32, low / len(cuts), high / len(cuts))
        loudness = loudness * jnp.repeat(jnp.exp(draws), dims[axis_at] // shards_of).reshape((-1,) + (1,) * (len(dims) - 1 - axis_at))
    return loudness


def profile(number_of, total, bound, slope):
    loads = [(1 << 20) // math.isqrt(rank ** slope) + 1 for rank in range(2, number_of + 1)]
    rest, counts = total - bound - (number_of - 1), [1] * (number_of - 1)
    while rest > 0:
        candidates = [i for i in range(number_of - 1) if counts[i] < bound]
        whole, budget = sum([loads[i] for i in candidates]), rest
        for i in candidates:
            extra = min(bound - counts[i], max(1, budget * loads[i] // whole), rest)
            counts[i] = counts[i] + extra
            rest = rest - extra
    return np.array([bound] + counts)


def ragged(own_key, number_of, total, most, slope):
    if number_of == 2:
        one = jax.random.randint(own_key, (), max(1, total - most), min(most, total - 1) + 1)
        return jnp.stack([one, total - one])
    sizes = jnp.asarray(profile(number_of, total, most, slope), jnp.int32)
    pairs = (number_of - 1) // 2
    source_of, receiver = sizes[1:1 + 2 * pairs:2], sizes[2:2 + 2 * pairs:2]
    margin = jnp.minimum(source_of - 1, most - receiver)
    moved = jax.random.randint(jax.random.fold_in(own_key, 1), (pairs,), 0, 1 << 20) % (margin + 1)
    sizes = sizes.at[1:1 + 2 * pairs:2].set(source_of - moved).at[2:2 + 2 * pairs:2].set(receiver + moved)
    return sizes[jax.random.permutation(jax.random.fold_in(own_key, 2), number_of)]


def normal_values(key, shape, scale, most, cuts=(), kind=jnp.bfloat16):
    array = scale * jax.random.normal(key, shape, jnp.float32)
    if cuts:
        array = array * block_levels(key, shape, cuts, -0.22, 0.18)
    return jnp.clip(array, -most, most).astype(kind)


def setup_inputs(seed: int = 0) -> dict:
    splits = jax.random.split(jax.random.key(seed), 14)
    return {
        "embeddings": normal_values(splits[0], (TILES, DIN), 1.0, 6.0, ((0, 128),)),
        "tile_position": draw_tile_position(jax.random.fold_in(splits[13], 71), 0),
        "w_in": normal_values(splits[2], (DIN, D), DIN ** -0.5, 0.15625),
        "ln_gain": jnp.clip(1.0 + 0.18 * jax.random.normal(splits[3], (D,), jnp.float32), 0.099609375, 1.8984375).astype(jnp.bfloat16),
        "w_query": draw_w_query(jax.random.fold_in(splits[13], 71), 0),
        "w_key": draw_w_key(jax.random.fold_in(splits[13], 71), 0),
        "w_value": normal_values(splits[6], (D, D), D ** -0.5, 0.21875),
        "w_out": normal_values(splits[7], (D, D), D ** -0.5, 0.21875),
        "near_lengths": jax.vmap(lambda own: ragged(own, NSEG_NEAR, SLIDE_LEN, NEAR_SPAN, 2))(jax.random.split(splits[8], SLIDES)).reshape((SLIDES, NSEG_NEAR)).astype(jnp.int32),
        "far_lengths": jax.vmap(lambda own: ragged(own, NSEG_FAR, SLIDE_LEN, ROWS, 2))(jax.random.split(splits[9], SLIDES)).reshape((SLIDES, NSEG_FAR)).astype(jnp.int32),
        "tissue": plant((jax.random.randint(splits[10], (TILES,), 0, 4) < 3).astype(jnp.int32), jax.random.fold_in(splits[10], 1), 0, 1),
        "hospital": draw_hospital(jax.random.fold_in(splits[13], 71), 0),
        "w_kernel": normal_values(splits[12], (D, P_SIZE), D ** -0.5, 0.21875, (), jnp.float32),
    }


NORM_EPSILON = 1e-05
MASKED_SCORE = -1e+30
GRAD_SCALE = 100.0

def layer_norm(inputs):
    center = inputs - lax.optimization_barrier(jnp.mean(inputs, axis=-1, keepdims=True))
    spread = lax.optimization_barrier(jnp.mean(center * center, axis=-1, keepdims=True))
    return center * lax.rsqrt(spread + NORM_EPSILON)

def segment_ids(positions, lengths):
    segment_ends = jnp.cumsum(lengths, dtype=jnp.int32)
    passed = (segment_ends <= positions[..., None]).astype(jnp.int32)
    return lax.optimization_barrier(jnp.sum(passed, axis=-1, dtype=jnp.int32))

def attend(queries, key_rows, values, query_pos, key_pos, query_seg, key_seg, slide_len):
    scaling = queries.shape[-1] ** (-0.5)
    scores = jnp.einsum('bqhe,bkhe->bhqk', queries.astype(jnp.float32), key_rows.astype(jnp.float32)) * scaling
    allowed = (query_seg[:, :, None] == key_seg[:, None, :]) & (key_pos[:, None, :] >= 0) & (key_pos[:, None, :] < slide_len)
    allowed = allowed[:, None, :, :]
    masked = jnp.where(allowed, scores, MASKED_SCORE)
    row_peak = lax.optimization_barrier(jnp.max(masked, axis=-1, keepdims=True))
    exponent = jnp.where(allowed, jnp.exp(masked - row_peak), 0.0)
    row_total = lax.optimization_barrier(jnp.sum(exponent, axis=-1, keepdims=True))
    weights = (exponent / row_total).astype(jnp.bfloat16)
    context = jnp.einsum('bhqk,bkhe->bqhe', weights.astype(jnp.float32), values.astype(jnp.float32))
    return context.astype(jnp.bfloat16)

def block_context(queries, near_kv, far_kv, base_pos, near_row, far_row, slide_len):
    tile_rows, width = queries.shape
    half_width = width // 2
    head_count = HEADS // 2
    head_size = width // HEADS
    near_span = tile_rows // 4
    half_rows = tile_rows // 2
    steps_near = jnp.arange(tile_rows, dtype=jnp.int32)
    near_query = queries[:, :half_width].reshape(2, half_rows, head_count, head_size)
    near_keys = jnp.stack([near_kv[0, :tile_rows], near_kv[0, half_rows:half_rows + tile_rows]]).reshape(2, tile_rows, head_count, head_size)
    near_values = jnp.stack([near_kv[1, :tile_rows], near_kv[1, half_rows:half_rows + tile_rows]]).reshape(2, tile_rows, head_count, head_size)
    query_pos = base_pos + steps_near.reshape(2, half_rows)
    key_pos = base_pos - near_span + jnp.stack([steps_near, steps_near + half_rows])
    near_context = attend(near_query, near_keys, near_values, query_pos, key_pos, segment_ids(query_pos, near_row), segment_ids(key_pos, near_row), slide_len)
    near_context = near_context.reshape(tile_rows, half_width)
    group_rows = tile_rows // DILATION
    far_query = queries[:, half_width:].reshape(group_rows, DILATION, head_count, head_size).transpose(1, 0, 2, 3)
    far_keys = far_kv[0].reshape(3 * group_rows, DILATION, head_count, head_size).transpose(1, 0, 2, 3)
    far_values = far_kv[1].reshape(3 * group_rows, DILATION, head_count, head_size).transpose(1, 0, 2, 3)
    offsets = jnp.arange(DILATION, dtype=jnp.int32)[:, None]
    far_query_pos = base_pos + DILATION * jnp.arange(group_rows, dtype=jnp.int32)[None, :] + offsets
    far_key_pos = base_pos - tile_rows + DILATION * jnp.arange(3 * group_rows, dtype=jnp.int32)[None, :] + offsets
    far_context = attend(far_query, far_keys, far_values, far_query_pos, far_key_pos, segment_ids(far_query_pos, far_row), segment_ids(far_key_pos, far_row), slide_len)
    far_context = far_context.transpose(1, 0, 2, 3).reshape(tile_rows, half_width)
    return jnp.concatenate([near_context, far_context], axis=1)

def gaussian(left, right):
    left_sq = lax.optimization_barrier(jnp.sum(left * left, axis=1))
    right_sq = lax.optimization_barrier(jnp.sum(right * right, axis=1))
    inner = jnp.dot(left, right.T, precision=lax.Precision.HIGHEST)
    return jnp.exp(-(left_sq[:, None] + right_sq[None, :] - 2.0 * inner) / (2.0 * left.shape[1]))

def reference(embeddings, tile_position, w_in, ln_gain, w_query, w_key, w_value, w_out, near_lengths, far_lengths, tissue, hospital, w_kernel):
    arrival = jnp.argsort(tile_position).astype(jnp.int32)
    slotted = embeddings[arrival]
    start_rows = jnp.dot(slotted, w_in, preferred_element_type=jnp.float32).astype(jnp.bfloat16)
    normed = (layer_norm(start_rows.astype(jnp.float32)) * ln_gain.astype(jnp.float32)).astype(jnp.bfloat16)
    queries = jnp.dot(normed, w_query, preferred_element_type=jnp.float32).astype(jnp.bfloat16)
    key_rows = jnp.dot(normed, w_key, preferred_element_type=jnp.float32).astype(jnp.bfloat16)
    values = jnp.dot(normed, w_value, preferred_element_type=jnp.float32).astype(jnp.bfloat16)
    query_slides = queries.reshape(SLIDES, SLIDE_LEN, D)
    key_value = jnp.stack([key_rows, values]).reshape(2, SLIDES, SLIDE_LEN, D)
    padded = jnp.pad(key_value, ((0, 0), (0, 0), (ROWS, ROWS), (0, 0)))
    zero_index = jnp.zeros((), jnp.int32)

    def one_block(device):
        slide_index = (device // N_REGION).astype(jnp.int32)
        base_pos = (device % N_REGION * ROWS).astype(jnp.int32)
        block_query = lax.dynamic_slice(query_slides, (slide_index, base_pos, zero_index), (1, ROWS, D))[0]
        window = lax.dynamic_slice(padded, (zero_index, slide_index, base_pos, zero_index), (2, 1, 3 * ROWS, D))[:, 0]
        near_kv = window[:, ROWS - NEAR_SPAN:2 * ROWS + NEAR_SPAN, :D // 2]
        far_kv = window[:, :, D // 2:]
        near_row = lax.dynamic_index_in_dim(near_lengths, slide_index, 0, keepdims=False)
        far_row = lax.dynamic_index_in_dim(far_lengths, slide_index, 0, keepdims=False)
        return block_context(block_query, near_kv, far_kv, base_pos, near_row, far_row, SLIDE_LEN)
    context = lax.map(one_block, jnp.arange(SENDERS, dtype=jnp.int32)).reshape(TILES, D)
    features = (start_rows.astype(jnp.float32) + jnp.dot(context, w_out, preferred_element_type=jnp.float32)).astype(jnp.bfloat16)
    tissue_rows = tissue.reshape(NREG, REGION).astype(jnp.float32)
    pooled = jnp.einsum('grd,gr->gd', features.reshape(NREG, REGION, D).astype(jnp.float32), tissue_rows) / REGION
    normal_pool = layer_norm(pooled)
    embedded = jnp.dot(normal_pool, w_kernel, precision=lax.Precision.HIGHEST)
    slide_of = jnp.arange(NREG, dtype=jnp.int32) // (REG_DEV * N_REGION)
    hospital_of = hospital[slide_of]
    count_one = jnp.sum(hospital_of).astype(jnp.float32)
    count_zero = jnp.sum(1 - hospital_of).astype(jnp.float32)
    weights = jnp.where(hospital_of == 1, 1.0 / count_one, -1.0 / count_zero).astype(jnp.float32)
    weighted = gaussian(embedded, embedded) * weights[None, :]
    kernel_sums = lax.optimization_barrier(jnp.sum(weighted, axis=1))
    moments = jnp.dot(weighted, embedded, precision=lax.Precision.HIGHEST)
    statistic = NREG * jnp.sum(weights * kernel_sums)
    grad_embedded = -2.0 * NREG / P_SIZE * weights[:, None] * (kernel_sums[:, None] * embedded - moments)
    kernel_grad = GRAD_SCALE * jnp.dot(normal_pool.T, grad_embedded, precision=lax.Precision.HIGHEST)
    return (features, statistic, kernel_grad)
```

```python
import functools

import jax
import jax.numpy as jnp
from jax import lax
from jax.experimental import pallas as pl
from jax.experimental.pallas import tpu as pltpu
from jax.sharding import PartitionSpec as P

MESH = pl.DeviceIdType.MESH
F32 = jnp.float32
BF16 = jnp.bfloat16
I32 = jnp.int32

ROWS = 1024
DIN = 1536
D = 768
PAIRS = 8
HEAD = 48
LANES = 128
PW = PAIRS // 2 * LANES
GROUP = 256
DIL = 4
REGION = 256
NENC = 4
NREGION = 32
PEERS = NENC * NREGION
CAP = 8
HALF = D // 2
EPS = 1e-05
BIG = 1e30
BITS = 9
PAD_SEG = 511
EXP_SCALE = 1.4426950408889634 / 48.0**0.5
VMEM_LIMIT = 56 * 1024 * 1024


def iota(shape, dim):
    return lax.broadcasted_iota(I32, shape, dim)


def dot(a, b):
    return jnp.dot(a, b, preferred_element_type=F32)


def params(**kw):
    return pltpu.CompilerParams(vmem_limit_bytes=VMEM_LIMIT, **kw)


VM = pl.BlockSpec(memory_space=pltpu.VMEM)


def project_kernel(emb_ref, pos_ref, w_ref, xs_ref, ps_ref, s_ref):
    pos = pos_ref[...].astype(F32)
    eye = iota((LANES, LANES), 0) == iota((LANES, LANES), 1)
    rank = jnp.zeros((1, ROWS), F32)
    for k in range(ROWS // LANES):
        part = pos[:, k * LANES : (k + 1) * LANES]
        col = jnp.sum(jnp.where(eye, part, 0.0), axis=1, keepdims=True)
        rank = rank + jnp.sum(jnp.where(col < pos, 1.0, 0.0), axis=0, keepdims=True)
    rank = rank.astype(I32)
    local = pos_ref[...] % ROWS
    slot = ((local % DIL) * GROUP + local // DIL).astype(F32)
    dest = iota((PEERS, ROWS), 0) * CAP
    lane = iota((PEERS, LANES), 1)
    table = jnp.zeros((PEERS, LANES), F32)
    for c in range(CAP):
        hit = jnp.where(dest + c == rank, slot, 0.0)
        table = jnp.where(lane == c, jnp.sum(hit, axis=1, keepdims=True), table)
    for d in range(PEERS):
        ps_ref[d] = table[d : d + 1, :]
    step = 256
    for k in range(ROWS // step):
        s_ref[pl.ds(k * step, step), :] = dot(
            emb_ref[pl.ds(k * step, step), :], w_ref[...]
        ).astype(BF16)
    for k in range(ROWS // step):
        pick = jnp.where(iota((step, ROWS), 0) + k * step == rank, 1.0, 0.0).astype(BF16)
        moved = dot(pick, s_ref[...]).reshape(step // CAP, CAP, D)
        both = jnp.concatenate([moved[:, :, :HALF], moved[:, :, HALF:]], axis=1)
        xs_ref[pl.ds(k * 2 * step, 2 * step), :] = both.reshape(2 * step, HALF).astype(BF16)


def exchange_kernel(xs_ref, ps_ref, xr_ref, pr_ref, sx, rx, sp, rp, own):
    me = lax.axis_index("enc") * NREGION + lax.axis_index("region")
    chunk = 2 * CAP
    barrier = pltpu.get_barrier_semaphore()

    def signal(k, carry):
        peer = (me + k) % PEERS
        pl.semaphore_signal(
            barrier, inc=1, device_id=(peer // NREGION, peer % NREGION), device_id_type=MESH
        )
        return carry

    lax.fori_loop(1, PEERS, signal, 0)
    mine_x = pltpu.make_async_copy(
        xs_ref.at[pl.ds(me * chunk, chunk), :], xr_ref.at[pl.ds(me * chunk, chunk), :], own.at[0]
    )
    mine_p = pltpu.make_async_copy(ps_ref.at[me], pr_ref.at[me], own.at[1])
    mine_x.start()
    mine_p.start()
    pl.semaphore_wait(barrier, PEERS - 1)

    def send(k, carry):
        peer = (me + k) % PEERS
        where = (peer // NREGION, peer % NREGION)
        pltpu.make_async_remote_copy(
            src_ref=ps_ref.at[peer], dst_ref=pr_ref.at[me],
            send_sem=sp, recv_sem=rp, device_id=where, device_id_type=MESH,
        ).start()
        pltpu.make_async_remote_copy(
            src_ref=xs_ref.at[pl.ds(peer * chunk, chunk), :],
            dst_ref=xr_ref.at[pl.ds(me * chunk, chunk), :],
            send_sem=sx, recv_sem=rx, device_id=where, device_id_type=MESH,
        ).start()
        return carry

    lax.fori_loop(1, PEERS, send, 0)
    mine_x.wait()
    mine_p.wait()
    rest_x = pl.ds(0, (PEERS - 1) * chunk)
    rest_p = pl.ds(0, PEERS - 1)
    pltpu.make_async_copy(ps_ref.at[rest_p], pr_ref.at[rest_p], rp).wait()
    pltpu.make_async_copy(ps_ref.at[rest_p], pr_ref.at[rest_p], sp).wait()
    pltpu.make_async_copy(xs_ref.at[rest_x, :], xr_ref.at[rest_x, :], rx).wait()
    pltpu.make_async_copy(xs_ref.at[rest_x, :], xr_ref.at[rest_x, :], sx).wait()


def land_kernel(xr_ref, pr_ref, gain_ref, start_ref, normed_ref, x_ref):
    table = jnp.concatenate([pr_ref[d] for d in range(PEERS)], axis=0)
    high = jnp.floor(table * (1.0 / 32.0))
    low = table - 32.0 * high
    spread = jnp.where(
        iota((LANES, ROWS), 0) == iota((LANES, ROWS), 1) % CAP, 1.0, 0.0
    ).astype(BF16)
    wide = 32.0 * dot(high.astype(BF16), spread) + dot(low.astype(BF16), spread)
    mine = iota((PEERS, ROWS), 0) == iota((PEERS, ROWS), 1) // CAP
    slot = jnp.sum(jnp.where(mine, wide, 0.0), axis=0, keepdims=True).astype(I32)
    step = 256
    for k in range(ROWS // step):
        got = xr_ref[pl.ds(k * 2 * step, 2 * step), :].astype(F32)
        got = got.reshape(step // CAP, 2 * CAP, HALF)
        both = jnp.concatenate([got[:, :CAP, :], got[:, CAP:, :]], axis=2)
        x_ref[pl.ds(k * step, step), :] = both.reshape(step, D).astype(BF16)
    gain = gain_ref[...].astype(F32)
    for k in range(ROWS // step):
        pick = jnp.where(iota((step, ROWS), 0) + k * step == slot, 1.0, 0.0).astype(BF16)
        rows = dot(pick, x_ref[...])
        start_ref[pl.ds(k * step, step), :] = rows.astype(BF16)
        center = rows - jnp.mean(rows, axis=1, keepdims=True)
        var = jnp.mean(center * center, axis=1, keepdims=True)
        normed_ref[pl.ds(k * step, step), :] = (center * lax.rsqrt(var + EPS) * gain).astype(BF16)


def ends_of(lengths):
    n = lengths.shape[1]
    upto = jnp.where(iota((n, n), 0) <= iota((n, n), 1), 1.0, 0.0).astype(BF16)
    high, low = lengths // 32, lengths % 32
    sums = 32.0 * dot(high.astype(F32).astype(BF16), upto) + dot(low.astype(F32).astype(BF16), upto)
    own = iota(sums.shape, 0) == lax.axis_index("enc")
    return jnp.sum(jnp.where(own, sums, 0.0), axis=0, keepdims=True)


def segment_of(pos, ends):
    seg = jnp.sum(jnp.where(ends <= pos.astype(F32), 1.0, 0.0), axis=1, keepdims=True).astype(I32)
    return jnp.where((pos >= 0) & (pos < ROWS * NREGION), seg, PAD_SEG)


def key_marks(seg):
    lane = iota((seg.shape[0], LANES), 1) - 2 * HEAD
    bit = (seg >> jnp.where(lane >= BITS, lane - BITS, jnp.maximum(lane, 0)) % 16) & 1
    mark = jnp.where(lane < BITS, 1 - bit, bit)
    return jnp.where((lane >= 0) & (lane < 2 * BITS), mark, 0).astype(F32)


def query_marks(seg):
    lane = iota((seg.shape[0], LANES), 1) - 2 * HEAD
    bit = (seg >> jnp.where(lane >= BITS, lane - BITS, jnp.maximum(lane, 0)) % 16) & 1
    mark = jnp.where(lane < BITS, bit, 1 - bit)
    return jnp.where((lane >= 0) & (lane < 2 * BITS), mark, 0).astype(F32) * -BIG


def attend(queries, marks, keys, values):
    n = queries.shape[0]
    lane = iota((n, LANES), 1)
    out = []
    for j in range(PAIRS // 2):
        cols = slice(j * LANES, (j + 1) * LANES)
        both = queries[:, cols]
        kk, vv = keys[:, cols], values[:, cols]
        parts = []
        for h in range(2):
            q = jnp.where((lane >= h * HEAD) & (lane < (h + 1) * HEAD), both, marks)
            s = lax.dot_general(q, kk, (((1,), (1,)), ((), ())), preferred_element_type=F32)
            peak = jnp.max(s, axis=1, keepdims=True)
            p = jnp.exp2((s - peak) * EXP_SCALE).astype(BF16)
            o = dot(p, vv)
            parts.append(o / o[:, 2 * HEAD : 2 * HEAD + 1])
        res = jnp.where(lane < HEAD, parts[0], jnp.where(lane < 2 * HEAD, parts[1], 0.0))
        out.append(res.astype(BF16))
    return jnp.concatenate(out, axis=1)


def layer_kernel(
    start_ref, own_ref, left_ref, right_ref, wq_ref, wk_ref, wv_ref, wo_ref,
    near_ref, far_ref, tissue_ref, feat_ref, pool_ref,
    q_ref, qm_ref, kn_ref, vn_ref, kf_ref, vf_ref, ctx_ref, nat_ref,
):
    base = lax.axis_index("region") * ROWS
    near_ends = ends_of(near_ref[...])
    far_ends = ends_of(far_ref[...])
    near_cols, far_cols = pl.ds(0, PW), pl.ds(PW, PW)
    ones_lane = jnp.where(iota((GROUP, PW), 1) % LANES == 2 * HEAD, 1.0, 0.0)

    def tiled(marks):
        return jnp.concatenate([marks] * (PAIRS // 2), axis=1)

    edge = GROUP // 4
    for o in range(DIL):
        rows = pl.ds(o * GROUP, GROUP)
        for b, ref in enumerate((left_ref, own_ref, right_ref)):
            x = ref[rows, :]
            pos = base + (b - 1) * ROWS + DIL * iota((GROUP, 1), 0) + o
            seg = segment_of(pos, far_ends)
            dst = pl.ds(b * GROUP, GROUP)
            kf_ref[o, dst, :] = (dot(x, wk_ref[:, far_cols]) + tiled(key_marks(seg))).astype(BF16)
            vf_ref[o, dst, :] = (dot(x, wv_ref[:, far_cols]) + ones_lane).astype(BF16)
            if b == 1:
                q_ref[rows, :] = dot(x, wq_ref[...]).astype(BF16)
                qm_ref[1, rows, :] = query_marks(seg).astype(BF16)
            first, count = ((GROUP - edge, edge), (0, GROUP), (0, edge))[b]
            to = (0, edge, edge + GROUP)[b]
            xn = ref[pl.ds(o * GROUP + first, count), :]
            npos = base + (b - 1) * ROWS + DIL * (iota((count, 1), 0) + first) + o
            nseg = segment_of(npos, near_ends)
            ndst = pl.ds(to, count)
            kn_ref[o, ndst, :] = (
                dot(xn, wk_ref[:, near_cols]) + tiled(key_marks(nseg))
            ).astype(BF16)
            vn_ref[o, ndst, :] = (dot(xn, wv_ref[:, near_cols]) + ones_lane[:count]).astype(BF16)
            if b == 1:
                qm_ref[0, rows, :] = query_marks(nseg).astype(BF16)

    def near_block(b, carry):
        g = pl.multiple_of(b * 32, 32)
        q = jnp.concatenate(
            [q_ref[pl.ds(o * GROUP + g, 32), near_cols] for o in range(DIL)], axis=0
        )
        m = jnp.concatenate([qm_ref[0, pl.ds(o * GROUP + g, 32), :] for o in range(DIL)], axis=0)
        k = jnp.concatenate([kn_ref[o, pl.ds(g, 160), :] for o in range(DIL)], axis=0)
        v = jnp.concatenate([vn_ref[o, pl.ds(g, 160), :] for o in range(DIL)], axis=0)
        out = attend(q, m, k, v)
        for o in range(DIL):
            ctx_ref[pl.ds(o * GROUP + g, 32), near_cols] = out[o * 32 : (o + 1) * 32, :]
        return carry

    lax.fori_loop(0, ROWS // 128, near_block, 0)

    def far_block(i, carry):
        o, half = i // 2, i % 2
        g = pl.multiple_of(half * 128, 128)
        rows = pl.ds(o * GROUP + g, 128)
        k = kf_ref[o, pl.ds(g, 640), :]
        v = vf_ref[o, pl.ds(g, 640), :]
        ctx_ref[rows, far_cols] = attend(q_ref[rows, far_cols], qm_ref[1, rows, :], k, v)
        return carry

    lax.fori_loop(0, ROWS // 128, far_block, 0)

    for o in range(DIL):
        rows = pl.ds(o * GROUP, GROUP)
        out = start_ref[rows, :].astype(F32) + dot(ctx_ref[rows, :], wo_ref[...])
        nat_ref[rows, :] = out.astype(BF16)
    step = 256
    for k in range(ROWS // step):
        r = iota((step, ROWS), 0) + k * step
        pick = jnp.where(
            iota((step, ROWS), 1) == (r % DIL) * GROUP + r // DIL, 1.0, 0.0
        ).astype(BF16)
        feat_ref[pl.ds(k * step, step), :] = dot(pick, nat_ref[...]).astype(BF16)
    sel = jnp.where(iota((8, ROWS), 0) == iota((8, ROWS), 1) // REGION, tissue_ref[...], 0)
    pooled = dot(sel.astype(BF16), feat_ref[...]) / REGION
    pool_ref[...] = pooled


AXES = ("x", "y", "z")


def region_kernel(pool_ref, hosp_ref, wk_ref, stat_ref, grad_ref, pair_ref, half_ref, full_ref, np_ref, ps, pr, ss, rs, cs, cr):
    enc, reg = lax.axis_index("enc"), lax.axis_index("region")
    core = reg % 2
    at = {"z": enc, "x": (reg // 2) % 4, "y": reg // 8}

    def device(shift):
        c = {a: (at[a] + shift.get(a, 0)) % 4 for a in AXES}
        return (c["z"], (c["y"] * 4 + c["x"]) * 2 + (core + shift.get("core", 0)) % 2)

    barrier = pltpu.get_barrier_semaphore()
    partners = [{"core": 1}] + [{a: k} for a in AXES for k in (1, 2, 3)]
    for shift in partners:
        pl.semaphore_signal(barrier, inc=1, device_id=device(shift), device_id_type=MESH)

    pooled = pool_ref[...]
    center = pooled - jnp.mean(pooled, axis=1, keepdims=True)
    var = jnp.mean(center * center, axis=1, keepdims=True)
    norm = center * lax.rsqrt(var + EPS)
    row = iota((8, D), 0)
    norm = jnp.where(row < 4, norm, 0.0)
    swapped = jnp.concatenate([norm[4:], norm[:4]], axis=0)
    pair_ref[0] = jnp.where(core == 0, norm, swapped)
    pl.semaphore_wait(barrier, len(partners))
    first = pltpu.make_async_remote_copy(
        src_ref=pair_ref.at[0], dst_ref=pair_ref.at[1], send_sem=ps, recv_sem=pr,
        device_id=device({"core": 1}), device_id_type=MESH,
    )
    first.start()
    first.wait()
    chip = pair_ref[0] + pair_ref[1]
    mine = jnp.where(core == 0, chip[:, :HALF], chip[:, HALF:])
    orders = [("z", "y", "x"), ("y", "x", "z"), ("x", "z", "y")]

    def offset(order):
        return ((at[order[2]] * 4 + at[order[1]]) * 4 + at[order[0]]) * 8

    for t, order in enumerate(orders):
        start = pl.multiple_of(offset(order), 8)
        half_ref[t, pl.ds(start, 8), :] = mine[:, t * LANES : (t + 1) * LANES]
    size = 8
    for stage in range(3):
        copies = []
        for t, order in enumerate(orders):
            start = pl.multiple_of(offset(order) // size * size, size)
            for k in (1, 2, 3):
                window = half_ref.at[t, pl.ds(start, size), :]
                copies.append(
                    pltpu.make_async_remote_copy(
                        src_ref=window, dst_ref=window,
                        send_sem=ss.at[stage, t, k - 1], recv_sem=rs.at[stage, t, k - 1],
                        device_id=device({order[stage]: k}), device_id_type=MESH,
                    )
                )
        for c in copies:
            c.start()
        for c in copies:
            c.wait()
        size *= 4
    last = pltpu.make_async_remote_copy(
        src_ref=half_ref, dst_ref=full_ref, send_sem=cs, recv_sem=cr,
        device_id=device({"core": 1}), device_id_type=MESH,
    )
    last.start()
    last.wait()

    for x in range(4):
        for y in range(4):
            for z in range(4):
                i = {"x": x, "y": y, "z": z}
                to = pl.ds(((x * 4 + y) * 4 + z) * 8, 8)
                for t, order in enumerate(orders):
                    src = pl.ds(((i[order[2]] * 4 + i[order[1]]) * 4 + i[order[0]]) * 8, 8)
                    a, b = half_ref[t, src, :], full_ref[t, src, :]
                    np_ref[to, t * LANES : (t + 1) * LANES] = jnp.where(core == 0, a, b)
                    np_ref[to, HALF + t * LANES : HALF + (t + 1) * LANES] = jnp.where(core == 0, b, a)

    n = PEERS * 4
    hp = lax.Precision.HIGHEST
    hosp = hosp_ref[...]
    ones = jnp.sum(hosp).astype(F32)
    per_slide = float(n // NENC)
    count_one = ones * per_slide
    count_zero = (NENC - ones) * per_slide

    def weights(slide, axis):
        label = jnp.zeros(slide.shape, I32)
        for s in range(NENC):
            label = jnp.where(slide == s, hosp[:, s : s + 1], label)
        return jnp.where(label == 1, 1.0 / count_one, -1.0 / count_zero)

    w_col = weights((iota((n, 1), 0) // 8) % 4, 0)
    w_row = weights((iota((1, n), 1) // 8) % 4, 1)
    normal = np_ref[...]
    emb = jnp.dot(normal, wk_ref[...], precision=hp, preferred_element_type=F32)
    sq = emb * emb
    sq_col = jnp.sum(sq, axis=1, keepdims=True)
    sq_row = lax.dot_general(
        jnp.ones((8, sq.shape[1]), F32), sq, (((1,), (1,)), ((), ())), precision=hp,
        preferred_element_type=F32,
    )[0:1, :]
    inner = lax.dot_general(
        emb, emb, (((1,), (1,)), ((), ())), precision=hp, preferred_element_type=F32
    )
    kern = jnp.exp(-(sq_col + sq_row - 2.0 * inner) / (2.0 * emb.shape[1])) * w_row
    sums = jnp.sum(kern, axis=1, keepdims=True)
    moments = jnp.dot(kern, emb, precision=hp, preferred_element_type=F32)
    stat = n * jnp.sum(w_col * sums)
    stat_ref[...] = jnp.zeros((8, LANES), F32) + stat
    g = (-2.0 * n / emb.shape[1]) * w_col * (sums * emb - moments)
    grad_ref[...] = 100.0 * lax.dot_general(
        normal, g, (((0,), (0,)), ((), ())), precision=hp, preferred_element_type=F32
    )


def pair_columns(w):
    w = w.reshape(w.shape[0], PAIRS, 2 * HEAD)
    return jnp.pad(w, ((0, 0), (0, 0), (0, LANES - 2 * HEAD))).reshape(w.shape[0], PAIRS * LANES)


def local(
    embeddings, tile_position, w_in, ln_gain, w_query, w_key, w_value, w_out,
    near_lengths, far_lengths, tissue, hospital, w_kernel,
):
    sds = jax.ShapeDtypeStruct
    xs, ps = pl.pallas_call(
        project_kernel,
        out_shape=(sds((2 * ROWS, HALF), BF16), sds((PEERS, 1, LANES), F32)),
        in_specs=[VM] * 3,
        out_specs=(VM, VM),
        scratch_shapes=[pltpu.VMEM((ROWS, D), BF16)],
        compiler_params=params(),
        name="project",
    )(embeddings, tile_position.reshape(1, ROWS), w_in)
    xr, pr = pl.pallas_call(
        exchange_kernel,
        out_shape=(sds((2 * ROWS, HALF), BF16), sds((PEERS, 1, LANES), F32)),
        in_specs=[VM] * 2,
        out_specs=(VM, VM),
        scratch_shapes=[pltpu.SemaphoreType.DMA] * 4 + [pltpu.SemaphoreType.DMA((2,))],
        compiler_params=params(collective_id=0, has_side_effects=True),
        name="exchange",
    )(xs, ps)
    start, normed = pl.pallas_call(
        land_kernel,
        out_shape=(sds((ROWS, D), BF16), sds((ROWS, D), BF16)),
        in_specs=[VM] * 3,
        out_specs=(VM, VM),
        scratch_shapes=[pltpu.VMEM((ROWS, D), BF16)],
        compiler_params=params(),
        name="land",
    )(xr, pr, ln_gain.reshape(1, D))
    up = [(i, i + 1) for i in range(NREGION - 1)]
    down = [(i + 1, i) for i in range(NREGION - 1)]
    left = lax.ppermute(normed, "region", up)
    right = lax.ppermute(normed, "region", down)

    wo = jnp.pad(
        w_out.reshape(PAIRS, 2 * HEAD, D), ((0, 0), (0, LANES - 2 * HEAD), (0, 0))
    ).reshape(PAIRS * LANES, D)
    features, pooled = pl.pallas_call(
        layer_kernel,
        out_shape=(sds((ROWS, D), BF16), sds((8, D), F32)),
        in_specs=[VM] * 11,
        out_specs=(VM, VM),
        scratch_shapes=[
            pltpu.VMEM((ROWS, 2 * PW), BF16),
            pltpu.VMEM((2, ROWS, LANES), BF16),
            pltpu.VMEM((DIL, GROUP + 128, PW), BF16),
            pltpu.VMEM((DIL, GROUP + 128, PW), BF16),
            pltpu.VMEM((DIL, 3 * GROUP, PW), BF16),
            pltpu.VMEM((DIL, 3 * GROUP, PW), BF16),
            pltpu.VMEM((ROWS, 2 * PW), BF16),
            pltpu.VMEM((ROWS, D), BF16),
        ],
        compiler_params=params(),
        name="layer",
    )(
        start, normed, left, right, pair_columns(w_query), pair_columns(w_key),
        pair_columns(w_value), wo, near_lengths, far_lengths, tissue.reshape(1, ROWS),
    )
    stat, grad = pl.pallas_call(
        region_kernel,
        out_shape=(sds((8, LANES), F32), sds((D, 256), F32)),
        in_specs=[VM] * 3,
        out_specs=(VM, VM),
        scratch_shapes=[
            pltpu.VMEM((2, 8, D), F32),
            pltpu.VMEM((3, 512, LANES), F32),
            pltpu.VMEM((3, 512, LANES), F32),
            pltpu.VMEM((512, D), F32),
            pltpu.SemaphoreType.DMA,
            pltpu.SemaphoreType.DMA,
            pltpu.SemaphoreType.DMA((3, 3, 3)),
            pltpu.SemaphoreType.DMA((3, 3, 3)),
            pltpu.SemaphoreType.DMA,
            pltpu.SemaphoreType.DMA,
        ],
        compiler_params=params(collective_id=1, has_side_effects=True),
        name="regions",
    )(pooled, hospital.reshape(1, NENC), w_kernel)
    return features, stat[0, 0], grad


def solution(mesh):
    split = P(("enc", "region"))
    return jax.shard_map(
        local,
        mesh=mesh,
        in_specs=(
            P(("enc", "region"), None), split, P(), P(), P(), P(), P(), P(), P(), P(), split, P(), P(),
        ),
        out_specs=(P(("enc", "region"), None), P(), P()),
        check_vma=False,
    )
```

```python
import functools

import jax
import jax.numpy as jnp
from jax import lax
from jax.experimental import pallas as pl
from jax.experimental.pallas import tpu as pltpu
from jax.sharding import PartitionSpec as P

MESH = pl.DeviceIdType.MESH
F32 = jnp.float32
BF16 = jnp.bfloat16
I32 = jnp.int32

ROWS = 1024
DIN = 1536
D = 768
PAIRS = 8
HEAD = 48
LANES = 128
PW = PAIRS // 2 * LANES
GROUP = 256
DIL = 4
REGION = 256
NENC = 4
NREGION = 32
PEERS = NENC * NREGION
CAP = 8
SPREAD = 45
HALF = D // 2
EPS = 1e-05
BIG = 1e30
BITS = 9
PAD_SEG = 511
EXP_SCALE = 1.4426950408889634 / 48.0**0.5
VMEM_LIMIT = 56 * 1024 * 1024


def iota(shape, dim):
    return lax.broadcasted_iota(I32, shape, dim)


def dot(a, b):
    return jnp.dot(a, b, preferred_element_type=F32)


def params(**kw):
    return pltpu.CompilerParams(vmem_limit_bytes=VMEM_LIMIT, **kw)


VM = pl.BlockSpec(memory_space=pltpu.VMEM)


def handoff_kernel(
    emb_ref, pos_ref, w_ref, gain_ref, wq_ref, wk_ref, wv_ref, wo_ref,
    start_ref, normed_ref, wq_out, wk_out, wv_out, wo_out,
    s_ref, tab_ref, xs_ref, ps_ref, xr_ref, pr_ref, sx, rx, sp, rp, own,
):
    me = lax.axis_index("enc") * NREGION + lax.axis_index("region")
    chunk = 2 * CAP
    barrier = pltpu.get_barrier_semaphore()

    def signal(k, carry):
        peer = (me + k) % PEERS
        pl.semaphore_signal(
            barrier, inc=1, device_id=(peer // NREGION, peer % NREGION), device_id_type=MESH
        )
        return carry

    lax.fori_loop(1, PEERS, signal, 0)

    pos = pos_ref[...].astype(F32)
    eye = iota((LANES, LANES), 0) == iota((LANES, LANES), 1)
    rank = jnp.zeros((1, ROWS), F32)
    for k in range(ROWS // LANES):
        part = pos[:, k * LANES : (k + 1) * LANES]
        col = jnp.sum(jnp.where(eye, part, 0.0), axis=1, keepdims=True)
        rank = rank + jnp.sum(jnp.where(col < pos, 1.0, 0.0), axis=0, keepdims=True)
    rank = rank.astype(I32)
    local = pos_ref[...] % ROWS
    slot = ((local % DIL) * GROUP + local // DIL).astype(F32)
    dest = iota((PEERS, ROWS), 0) * CAP
    lane = iota((PEERS, LANES), 1)
    table = jnp.zeros((PEERS, LANES), F32)
    for c in range(CAP):
        hit = jnp.where(dest + c == rank, slot, 0.0)
        table = jnp.where(lane == c, jnp.sum(hit, axis=1, keepdims=True), table)
    tab_ref[...] = table

    def spill(d, carry):
        ps_ref[d] = tab_ref[pl.ds(d, 1), :]
        return carry

    lax.fori_loop(0, PEERS, spill, 0)
    step = 256
    for k in range(ROWS // step):
        s_ref[pl.ds(k * step, step), :] = dot(
            emb_ref[pl.ds(k * step, step), :], w_ref[...]
        ).astype(BF16)
    for k in range(ROWS // step):
        pick = jnp.where(iota((step, ROWS), 0) + k * step == rank, 1.0, 0.0).astype(BF16)
        moved = dot(pick, s_ref[...]).reshape(step // CAP, CAP, D)
        both = jnp.concatenate([moved[:, :, :HALF], moved[:, :, HALF:]], axis=1)
        xs_ref[pl.ds(k * 2 * step, 2 * step), :] = both.reshape(2 * step, HALF).astype(BF16)

    mine_x = pltpu.make_async_copy(
        xs_ref.at[pl.ds(me * chunk, chunk), :], xr_ref.at[pl.ds(me * chunk, chunk), :], own.at[0]
    )
    mine_p = pltpu.make_async_copy(ps_ref.at[me], pr_ref.at[me], own.at[1])
    mine_x.start()
    mine_p.start()
    pl.semaphore_wait(barrier, PEERS - 1)

    def send(k, carry):
        peer = (me + k * SPREAD) % PEERS
        where = (peer // NREGION, peer % NREGION)
        pltpu.make_async_remote_copy(
            src_ref=ps_ref.at[peer], dst_ref=pr_ref.at[me],
            send_sem=sp, recv_sem=rp, device_id=where, device_id_type=MESH,
        ).start()
        pltpu.make_async_remote_copy(
            src_ref=xs_ref.at[pl.ds(peer * chunk, chunk), :],
            dst_ref=xr_ref.at[pl.ds(me * chunk, chunk), :],
            send_sem=sx, recv_sem=rx, device_id=where, device_id_type=MESH,
        ).start()
        return carry

    lax.fori_loop(1, PEERS, send, 0)

    gap = jnp.zeros((D, LANES - 2 * HEAD), BF16)
    for src, dst in ((wq_ref, wq_out), (wk_ref, wk_out), (wv_ref, wv_out)):
        for j in range(PAIRS):
            pair = src[:, 2 * HEAD * j : 2 * HEAD * (j + 1)]
            dst[:, LANES * j : LANES * (j + 1)] = jnp.concatenate([pair, gap], axis=1)
    for j in range(PAIRS):
        wo_out[pl.ds(LANES * j, 2 * HEAD), :] = wo_ref[pl.ds(2 * HEAD * j, 2 * HEAD), :]
        wo_out[pl.ds(LANES * j + 2 * HEAD, LANES - 2 * HEAD), :] = jnp.zeros((LANES - 2 * HEAD, D), BF16)

    mine_x.wait()
    mine_p.wait()
    rest_x = pl.ds(0, (PEERS - 1) * chunk)
    rest_p = pl.ds(0, PEERS - 1)
    pltpu.make_async_copy(ps_ref.at[rest_p], pr_ref.at[rest_p], rp).wait()
    pltpu.make_async_copy(ps_ref.at[rest_p], pr_ref.at[rest_p], sp).wait()

    def fill(d, carry):
        tab_ref[pl.ds(d, 1), :] = pr_ref[d]
        return carry

    lax.fori_loop(0, PEERS, fill, 0)
    table = tab_ref[...]
    high = jnp.floor(table * (1.0 / 32.0))
    low = table - 32.0 * high
    spread = jnp.where(
        iota((LANES, ROWS), 0) == iota((LANES, ROWS), 1) % CAP, 1.0, 0.0
    ).astype(BF16)
    wide = 32.0 * dot(high.astype(BF16), spread) + dot(low.astype(BF16), spread)
    mine = iota((PEERS, ROWS), 0) == iota((PEERS, ROWS), 1) // CAP
    place = jnp.sum(jnp.where(mine, wide, 0.0), axis=0, keepdims=True).astype(I32)

    pltpu.make_async_copy(xs_ref.at[rest_x, :], xr_ref.at[rest_x, :], rx).wait()
    pltpu.make_async_copy(xs_ref.at[rest_x, :], xr_ref.at[rest_x, :], sx).wait()
    for k in range(ROWS // step):
        got = xr_ref[pl.ds(k * 2 * step, 2 * step), :].astype(F32)
        got = got.reshape(step // CAP, 2 * CAP, HALF)
        both = jnp.concatenate([got[:, :CAP, :], got[:, CAP:, :]], axis=2)
        s_ref[pl.ds(k * step, step), :] = both.reshape(step, D).astype(BF16)
    gain = gain_ref[...].astype(F32)
    for k in range(ROWS // step):
        pick = jnp.where(iota((step, ROWS), 0) + k * step == place, 1.0, 0.0).astype(BF16)
        rows = dot(pick, s_ref[...])
        start_ref[pl.ds(k * step, step), :] = rows.astype(BF16)
        center = rows - jnp.mean(rows, axis=1, keepdims=True)
        var = jnp.mean(center * center, axis=1, keepdims=True)
        normed_ref[pl.ds(k * step, step), :] = (center * lax.rsqrt(var + EPS) * gain).astype(BF16)


def ends_of(lengths):
    n = lengths.shape[1]
    upto = jnp.where(iota((n, n), 0) <= iota((n, n), 1), 1.0, 0.0).astype(BF16)
    high, low = lengths // 32, lengths % 32
    sums = 32.0 * dot(high.astype(F32).astype(BF16), upto) + dot(low.astype(F32).astype(BF16), upto)
    own = iota(sums.shape, 0) == lax.axis_index("enc")
    return jnp.sum(jnp.where(own, sums, 0.0), axis=0, keepdims=True)


def segment_of(pos, ends):
    seg = jnp.sum(jnp.where(ends <= pos.astype(F32), 1.0, 0.0), axis=1, keepdims=True).astype(I32)
    return jnp.where((pos >= 0) & (pos < ROWS * NREGION), seg, PAD_SEG)


def key_marks(seg):
    lane = iota((seg.shape[0], LANES), 1) - 2 * HEAD
    bit = (seg >> jnp.where(lane >= BITS, lane - BITS, jnp.maximum(lane, 0)) % 16) & 1
    mark = jnp.where(lane < BITS, 1 - bit, bit)
    return jnp.where((lane >= 0) & (lane < 2 * BITS), mark, 0).astype(F32)


def query_marks(seg):
    lane = iota((seg.shape[0], LANES), 1) - 2 * HEAD
    bit = (seg >> jnp.where(lane >= BITS, lane - BITS, jnp.maximum(lane, 0)) % 16) & 1
    mark = jnp.where(lane < BITS, bit, 1 - bit)
    return jnp.where((lane >= 0) & (lane < 2 * BITS), mark, 0).astype(F32) * -BIG


def attend(query, marks, key, value):
    n = marks.shape[0]
    lane = iota((n, LANES), 1)
    pairs = range(PAIRS // 2)
    scores = []
    for j in pairs:
        both = query(j)
        q = jnp.concatenate(
            [
                jnp.where((lane >= h * HEAD) & (lane < (h + 1) * HEAD), both, marks)
                for h in range(2)
            ],
            axis=0,
        )
        scores.append(
            lax.dot_general(q, key(j), (((1,), (1,)), ((), ())), preferred_element_type=F32)
        )
    probs = [
        jnp.exp2((s - jnp.max(s, axis=1, keepdims=True)) * EXP_SCALE).astype(BF16) for s in scores
    ]
    out = []
    for j in pairs:
        o = dot(probs[j], value(j))
        o = o / o[:, 2 * HEAD : 2 * HEAD + 1]
        o = jnp.where(lane < HEAD, o[:n], jnp.where(lane < 2 * HEAD, o[n:], 0.0))
        out.append(o.astype(BF16))
    return jnp.concatenate(out, axis=1)


def layer_kernel(
    start_ref, own_ref, wq_ref, wk_ref, wv_ref, wo_ref,
    near_ref, far_ref, tissue_ref, feat_ref, pool_ref,
    left_ref, right_ref, q_ref, qm_ref, kn_ref, vn_ref, kf_ref, vf_ref, ctx_ref, nat_ref,
    send_sem, recv_sem,
):
    enc, reg = lax.axis_index("enc"), lax.axis_index("region")
    after, before = (reg + 1) % NREGION, (reg + NREGION - 1) % NREGION
    barrier = pltpu.get_barrier_semaphore()
    for other in (before, after):
        pl.semaphore_signal(barrier, inc=1, device_id=(enc, other), device_id_type=MESH)
    pl.semaphore_wait(barrier, 2)
    edge = GROUP // 4
    near_copies, far_copies = [], []
    for kind, copies in ((0, near_copies), (1, far_copies)):
        for o in range(DIL):
            for way, dst, other in ((0, left_ref, after), (1, right_ref, before)):
                first = ((GROUP - edge, 0), (0, edge))[kind][way]
                rows = pl.ds(o * GROUP + first, (edge, GROUP - edge)[kind])
                copies.append(
                    pltpu.make_async_remote_copy(
                        src_ref=own_ref.at[rows, :], dst_ref=dst.at[rows, :],
                        send_sem=send_sem.at[kind, way, o], recv_sem=recv_sem.at[kind, way, o],
                        device_id=(enc, other), device_id_type=MESH,
                    )
                )
    for c in near_copies:
        c.start()
    for c in far_copies:
        c.start()

    base = reg * ROWS
    near_ends = ends_of(near_ref[...])
    far_ends = ends_of(far_ref[...])
    near_cols, far_cols = pl.ds(0, PW), pl.ds(PW, PW)
    ones_lane = jnp.where(iota((GROUP, PW), 1) % LANES == 2 * HEAD, 1.0, 0.0)

    def tiled(marks):
        return jnp.concatenate([marks] * (PAIRS // 2), axis=1)

    def far_rows(o, b, ref):
        x = ref[pl.ds(o * GROUP, GROUP), :]
        seg = segment_of(base + (b - 1) * ROWS + DIL * iota((GROUP, 1), 0) + o, far_ends)
        dst = pl.ds(b * GROUP, GROUP)
        kf_ref[o, dst, :] = (dot(x, wk_ref[:, far_cols]) + tiled(key_marks(seg))).astype(BF16)
        vf_ref[o, dst, :] = (dot(x, wv_ref[:, far_cols]) + ones_lane).astype(BF16)
        return seg

    def near_rows(o, b, ref):
        first, count = ((GROUP - edge, edge), (0, GROUP), (0, edge))[b]
        x = ref[pl.ds(o * GROUP + first, count), :]
        pos = base + (b - 1) * ROWS + DIL * (iota((count, 1), 0) + first) + o
        seg = segment_of(pos, near_ends)
        dst = pl.ds((0, edge, edge + GROUP)[b], count)
        kn_ref[o, dst, :] = (dot(x, wk_ref[:, near_cols]) + tiled(key_marks(seg))).astype(BF16)
        vn_ref[o, dst, :] = (dot(x, wv_ref[:, near_cols]) + ones_lane[:count]).astype(BF16)
        return seg

    for o in range(DIL):
        rows = pl.ds(o * GROUP, GROUP)
        q_ref[rows, :] = dot(own_ref[rows, :], wq_ref[...]).astype(BF16)
        qm_ref[0, rows, :] = query_marks(near_rows(o, 1, own_ref)).astype(BF16)
        qm_ref[1, rows, :] = query_marks(far_rows(o, 1, own_ref)).astype(BF16)
    for c in near_copies:
        c.wait()
    for o in range(DIL):
        near_rows(o, 0, left_ref)
        near_rows(o, 2, right_ref)

    def near_block(b, carry):
        g = pl.multiple_of(b * 32, 32)

        def joined(ref, n, j):
            cols = slice(j * LANES, (j + 1) * LANES)
            return jnp.concatenate([ref[o, pl.ds(g, n), cols] for o in range(DIL)], axis=0)

        def query(j):
            cols = slice(j * LANES, (j + 1) * LANES)
            return jnp.concatenate(
                [q_ref[pl.ds(o * GROUP + g, 32), cols] for o in range(DIL)], axis=0
            )

        marks = jnp.concatenate(
            [qm_ref[0, pl.ds(o * GROUP + g, 32), :] for o in range(DIL)], axis=0
        )
        out = attend(query, marks, lambda j: joined(kn_ref, 160, j), lambda j: joined(vn_ref, 160, j))
        for o in range(DIL):
            ctx_ref[pl.ds(o * GROUP + g, 32), near_cols] = out[o * 32 : (o + 1) * 32, :]
        return carry

    lax.fori_loop(0, ROWS // 128, near_block, 0)
    for c in far_copies:
        c.wait()
    for o in range(DIL):
        far_rows(o, 0, left_ref)
        far_rows(o, 2, right_ref)

    def far_block(i, carry):
        o, half = i // 2, i % 2
        g = pl.multiple_of(half * 128, 128)
        rows = pl.ds(pl.multiple_of(o * GROUP + g, 128), 128)
        ctx_ref[rows, far_cols] = attend(
            lambda j: q_ref[rows, PW + j * LANES : PW + (j + 1) * LANES],
            qm_ref[1, rows, :],
            lambda j: kf_ref[o, pl.ds(g, 640), j * LANES : (j + 1) * LANES],
            lambda j: vf_ref[o, pl.ds(g, 640), j * LANES : (j + 1) * LANES],
        )
        return carry

    lax.fori_loop(0, ROWS // 128, far_block, 0)

    for o in range(DIL):
        rows = pl.ds(o * GROUP, GROUP)
        out = start_ref[rows, :].astype(F32) + dot(ctx_ref[rows, :], wo_ref[...])
        nat_ref[rows, :] = out.astype(BF16)
    step = 256
    for k in range(ROWS // step):
        r = iota((step, ROWS), 0) + k * step
        pick = jnp.where(
            iota((step, ROWS), 1) == (r % DIL) * GROUP + r // DIL, 1.0, 0.0
        ).astype(BF16)
        feat_ref[pl.ds(k * step, step), :] = dot(pick, nat_ref[...]).astype(BF16)
    sel = jnp.where(
        iota((8, ROWS), 0) == iota((8, ROWS), 1) // REGION, tissue_ref[...], 0
    )
    pool_ref[...] = dot(sel.astype(F32).astype(BF16), feat_ref[...]) / REGION


AXES = ("x", "y", "z")


def region_kernel(pool_ref, hosp_ref, wk_ref, stat_ref, grad_ref, pair_ref, half_ref, full_ref, np_ref, ps, pr, ss, rs, cs, cr):
    enc, reg = lax.axis_index("enc"), lax.axis_index("region")
    core = reg % 2
    at = {"z": enc, "x": (reg // 2) % 4, "y": reg // 8}

    def device(shift):
        c = {a: (at[a] + shift.get(a, 0)) % 4 for a in AXES}
        return (c["z"], (c["y"] * 4 + c["x"]) * 2 + (core + shift.get("core", 0)) % 2)

    barrier = pltpu.get_barrier_semaphore()
    partners = [{"core": 1}] + [{a: k} for a in AXES for k in (1, 2, 3)]
    for shift in partners:
        pl.semaphore_signal(barrier, inc=1, device_id=device(shift), device_id_type=MESH)

    pooled = pool_ref[...]
    center = pooled - jnp.mean(pooled, axis=1, keepdims=True)
    var = jnp.mean(center * center, axis=1, keepdims=True)
    norm = center * lax.rsqrt(var + EPS)
    row = iota((8, D), 0)
    norm = jnp.where(row < 4, norm, 0.0)
    swapped = jnp.concatenate([norm[4:], norm[:4]], axis=0)
    pair_ref[0] = jnp.where(core == 0, norm, swapped)
    pl.semaphore_wait(barrier, len(partners))
    first = pltpu.make_async_remote_copy(
        src_ref=pair_ref.at[0], dst_ref=pair_ref.at[1], send_sem=ps, recv_sem=pr,
        device_id=device({"core": 1}), device_id_type=MESH,
    )
    first.start()
    first.wait()
    chip = pair_ref[0] + pair_ref[1]
    mine = jnp.where(core == 0, chip[:, :HALF], chip[:, HALF:])
    orders = [("z", "y", "x"), ("y", "x", "z"), ("x", "z", "y")]

    def offset(order):
        return ((at[order[2]] * 4 + at[order[1]]) * 4 + at[order[0]]) * 8

    for t, order in enumerate(orders):
        start = pl.multiple_of(offset(order), 8)
        half_ref[t, pl.ds(start, 8), :] = mine[:, t * LANES : (t + 1) * LANES]
    size = 8
    for stage in range(3):
        copies = []
        for t, order in enumerate(orders):
            start = pl.multiple_of(offset(order) // size * size, size)
            for k in (1, 2, 3):
                window = half_ref.at[t, pl.ds(start, size), :]
                copies.append(
                    pltpu.make_async_remote_copy(
                        src_ref=window, dst_ref=window,
                        send_sem=ss.at[stage, t, k - 1], recv_sem=rs.at[stage, t, k - 1],
                        device_id=device({order[stage]: k}), device_id_type=MESH,
                    )
                )
        for c in copies:
            c.start()
        for c in copies:
            c.wait()
        size *= 4
    last = pltpu.make_async_remote_copy(
        src_ref=half_ref, dst_ref=full_ref, send_sem=cs, recv_sem=cr,
        device_id=device({"core": 1}), device_id_type=MESH,
    )
    last.start()
    last.wait()

    for x in range(4):
        for y in range(4):
            for z in range(4):
                i = {"x": x, "y": y, "z": z}
                to = pl.ds(((x * 4 + y) * 4 + z) * 8, 8)
                for t, order in enumerate(orders):
                    src = pl.ds(((i[order[2]] * 4 + i[order[1]]) * 4 + i[order[0]]) * 8, 8)
                    a, b = half_ref[t, src, :], full_ref[t, src, :]
                    np_ref[to, t * LANES : (t + 1) * LANES] = jnp.where(core == 0, a, b)
                    np_ref[to, HALF + t * LANES : HALF + (t + 1) * LANES] = jnp.where(core == 0, b, a)

    n = PEERS * 4
    hp = lax.Precision.HIGHEST
    hosp = hosp_ref[...]
    ones = jnp.sum(hosp).astype(F32)
    per_slide = float(n // NENC)
    count_one = ones * per_slide
    count_zero = (NENC - ones) * per_slide

    def weights(slide, axis):
        label = jnp.zeros(slide.shape, I32)
        for s in range(NENC):
            label = jnp.where(slide == s, hosp[:, s : s + 1], label)
        return jnp.where(label == 1, 1.0 / count_one, -1.0 / count_zero)

    w_col = weights((iota((n, 1), 0) // 8) % 4, 0)
    w_row = weights((iota((1, n), 1) // 8) % 4, 1)
    normal = np_ref[...]
    emb = jnp.dot(normal, wk_ref[...], precision=hp, preferred_element_type=F32)
    sq = emb * emb
    sq_col = jnp.sum(sq, axis=1, keepdims=True)
    sq_row = lax.dot_general(
        jnp.ones((8, sq.shape[1]), F32), sq, (((1,), (1,)), ((), ())), precision=hp,
        preferred_element_type=F32,
    )[0:1, :]
    inner = lax.dot_general(
        emb, emb, (((1,), (1,)), ((), ())), precision=hp, preferred_element_type=F32
    )
    kern = jnp.exp(-(sq_col + sq_row - 2.0 * inner) / (2.0 * emb.shape[1])) * w_row
    sums = jnp.sum(kern, axis=1, keepdims=True)
    moments = jnp.dot(kern, emb, precision=hp, preferred_element_type=F32)
    stat = n * jnp.sum(w_col * sums)
    stat_ref[...] = jnp.zeros((8, LANES), F32) + stat
    g = (-2.0 * n / emb.shape[1]) * w_col * (sums * emb - moments)
    grad_ref[...] = 100.0 * lax.dot_general(
        normal, g, (((0,), (0,)), ((), ())), precision=hp, preferred_element_type=F32
    )


def local(
    embeddings, tile_position, w_in, ln_gain, w_query, w_key, w_value, w_out,
    near_lengths, far_lengths, tissue, hospital, w_kernel,
):
    sds = jax.ShapeDtypeStruct
    dma = pltpu.SemaphoreType.DMA
    rows, padded = sds((ROWS, D), BF16), sds((D, PAIRS * LANES), BF16)
    start, normed, wq, wk, wv, wo = pl.pallas_call(
        handoff_kernel,
        out_shape=(rows, rows, padded, padded, padded, sds((PAIRS * LANES, D), BF16)),
        in_specs=[VM] * 8,
        out_specs=(VM,) * 6,
        scratch_shapes=[
            pltpu.VMEM((ROWS, D), BF16),
            pltpu.VMEM((PEERS, LANES), F32),
            pltpu.VMEM((2 * ROWS, HALF), BF16),
            pltpu.VMEM((PEERS, 1, LANES), F32),
            pltpu.VMEM((2 * ROWS, HALF), BF16),
            pltpu.VMEM((PEERS, 1, LANES), F32),
            dma, dma, dma, dma, dma((2,)),
        ],
        compiler_params=params(collective_id=0, has_side_effects=True),
        name="handoff",
    )(
        embeddings, tile_position.reshape(1, ROWS), w_in, ln_gain.reshape(1, D),
        w_query, w_key, w_value, w_out,
    )
    features, pooled = pl.pallas_call(
        layer_kernel,
        out_shape=(rows, sds((8, D), F32)),
        in_specs=[VM] * 9,
        out_specs=(VM, VM),
        scratch_shapes=[
            pltpu.VMEM((ROWS, D), BF16),
            pltpu.VMEM((ROWS, D), BF16),
            pltpu.VMEM((ROWS, 2 * PW), BF16),
            pltpu.VMEM((2, ROWS, LANES), BF16),
            pltpu.VMEM((DIL, GROUP + 128, PW), BF16),
            pltpu.VMEM((DIL, GROUP + 128, PW), BF16),
            pltpu.VMEM((DIL, 3 * GROUP, PW), BF16),
            pltpu.VMEM((DIL, 3 * GROUP, PW), BF16),
            pltpu.VMEM((ROWS, 2 * PW), BF16),
            pltpu.VMEM((ROWS, D), BF16),
            dma((2, 2, DIL)),
            dma((2, 2, DIL)),
        ],
        compiler_params=params(collective_id=2, has_side_effects=True),
        name="layer",
    )(start, normed, wq, wk, wv, wo, near_lengths, far_lengths, tissue.reshape(1, ROWS))
    stat, grad = pl.pallas_call(
        region_kernel,
        out_shape=(sds((8, LANES), F32), sds((D, 256), F32)),
        in_specs=[VM] * 3,
        out_specs=(VM, VM),
        scratch_shapes=[
            pltpu.VMEM((2, 8, D), F32),
            pltpu.VMEM((3, 512, LANES), F32),
            pltpu.VMEM((3, 512, LANES), F32),
            pltpu.VMEM((512, D), F32),
            pltpu.SemaphoreType.DMA,
            pltpu.SemaphoreType.DMA,
            pltpu.SemaphoreType.DMA((3, 3, 3)),
            pltpu.SemaphoreType.DMA((3, 3, 3)),
            pltpu.SemaphoreType.DMA,
            pltpu.SemaphoreType.DMA,
        ],
        compiler_params=params(collective_id=1, has_side_effects=True),
        name="regions",
    )(pooled, hospital.reshape(1, NENC), w_kernel)
    return features, stat[0, 0], grad


def solution(mesh):
    split = P(("enc", "region"))
    return jax.shard_map(
        local,
        mesh=mesh,
        in_specs=(
            P(("enc", "region"), None), split, P(), P(), P(), P(), P(), P(), P(), P(), split, P(), P(),
        ),
        out_specs=(P(("enc", "region"), None), P(), P()),
        check_vma=False,
    )
```

```python
import functools

import jax
import jax.numpy as jnp
from jax import lax
from jax.experimental import pallas as pl
from jax.experimental.pallas import tpu as pltpu
from jax.sharding import PartitionSpec as P

MESH = pl.DeviceIdType.MESH
F32 = jnp.float32
BF16 = jnp.bfloat16
I32 = jnp.int32

ROWS = 1024
DIN = 1536
D = 768
PAIRS = 8
HEAD = 48
LANES = 128
PW = PAIRS // 2 * LANES
GROUP = 256
DIL = 4
REGION = 256
NENC = 4
NREGION = 32
PEERS = NENC * NREGION
CAP = 8
SPREAD = 45
HALF = D // 2
EPS = 1e-05
BIG = 1e30
BITS = 9
PAD_SEG = 511
EXP_SCALE = 1.4426950408889634 / 48.0**0.5
VMEM_LIMIT = 60 * 1024 * 1024


def iota(shape, dim):
    return lax.broadcasted_iota(I32, shape, dim)


def dot(a, b):
    return jnp.dot(a, b, preferred_element_type=F32)


def params(**kw):
    return pltpu.CompilerParams(vmem_limit_bytes=VMEM_LIMIT, **kw)


VM = pl.BlockSpec(memory_space=pltpu.VMEM)
ANY = pl.BlockSpec(memory_space=pl.ANY)


def ends_of(lengths):
    n = lengths.shape[1]
    upto = jnp.where(iota((n, n), 0) <= iota((n, n), 1), 1.0, 0.0).astype(BF16)
    high, low = lengths // 32, lengths % 32
    sums = 32.0 * dot(high.astype(F32).astype(BF16), upto) + dot(low.astype(F32).astype(BF16), upto)
    own = iota(sums.shape, 0) == lax.axis_index("enc")
    return jnp.sum(jnp.where(own, sums, 0.0), axis=0, keepdims=True)


def segment_of(pos, ends):
    seg = jnp.sum(jnp.where(ends <= pos.astype(F32), 1.0, 0.0), axis=1, keepdims=True).astype(I32)
    return jnp.where((pos >= 0) & (pos < ROWS * NREGION), seg, PAD_SEG)


def key_marks(seg):
    lane = iota((seg.shape[0], LANES), 1) - 2 * HEAD
    bit = (seg >> jnp.where(lane >= BITS, lane - BITS, jnp.maximum(lane, 0)) % 16) & 1
    mark = jnp.where(lane < BITS, 1 - bit, bit)
    return jnp.where((lane >= 0) & (lane < 2 * BITS), mark, 0).astype(F32)


def query_marks(seg):
    lane = iota((seg.shape[0], LANES), 1) - 2 * HEAD
    bit = (seg >> jnp.where(lane >= BITS, lane - BITS, jnp.maximum(lane, 0)) % 16) & 1
    mark = jnp.where(lane < BITS, bit, 1 - bit)
    return jnp.where((lane >= 0) & (lane < 2 * BITS), mark, 0).astype(F32) * -BIG


def attend(query, marks, key, value):
    n = marks.shape[0]
    lane = iota((n, LANES), 1)
    pairs = range(PAIRS // 2)
    scores = []
    for j in pairs:
        both = query(j)
        q = jnp.concatenate(
            [
                jnp.where((lane >= h * HEAD) & (lane < (h + 1) * HEAD), both, marks)
                for h in range(2)
            ],
            axis=0,
        )
        scores.append(
            lax.dot_general(q, key(j), (((1,), (1,)), ((), ())), preferred_element_type=F32)
        )
    probs = [
        jnp.exp2((s - jnp.max(s, axis=1, keepdims=True)) * EXP_SCALE).astype(BF16) for s in scores
    ]
    out = []
    for j in pairs:
        o = dot(probs[j], value(j))
        o = o / o[:, 2 * HEAD : 2 * HEAD + 1]
        o = jnp.where(lane < HEAD, o[:n], jnp.where(lane < 2 * HEAD, o[n:], 0.0))
        out.append(o.astype(BF16))
    return jnp.concatenate(out, axis=1)


AXES = ("x", "y", "z")


def dot3(a, b, ca=1, cb=0):
    dims = (((ca,), (cb,)), ((), ()))

    def mul(x, y):
        return lax.dot_general(x, y, dims, preferred_element_type=F32)

    ah, bh = a.astype(BF16), b.astype(BF16)
    al, bl = (a - ah.astype(F32)).astype(BF16), (b - bh.astype(F32)).astype(BF16)
    return mul(ah, bh) + (mul(ah, bl) + mul(al, bh))


def slide_kernel(
    emb_hbm, pos_ref, win_hbm, gain_ref, wq_hbm, wk_hbm, wv_hbm, wo_hbm,
    near_ref, far_ref, tissue_ref, hosp_ref, wkern_hbm,
    feat_hbm, stat_ref, grad_ref,
    emb_ref, w_ref, wq_ref, wk_ref, wv_ref, wo_ref, wkern_ref, wq_out, wk_out, wv_out, wo_out,
    start_ref, normed_ref, s_ref, tab_ref, xs_ref, ps_ref, xr_ref, pr_ref,
    left_ref, right_ref, q_ref, qm_ref, kn_ref, vn_ref, kf_ref, vf_ref, ctx_ref,
    pair_ref, half_ref, full_ref, np_ref,
    load_sem, sx, rx, sp, rp, own, send_sem, recv_sem, ps, pr, ss, rs, cs, cr,
):
    me = lax.axis_index("enc") * NREGION + lax.axis_index("region")
    chunk = 2 * CAP
    barrier = pltpu.get_barrier_semaphore()

    def signal(k, carry):
        peer = (me + k) % PEERS
        pl.semaphore_signal(
            barrier, inc=1, device_id=(peer // NREGION, peer % NREGION), device_id_type=MESH
        )
        return carry

    lax.fori_loop(1, PEERS, signal, 0)
    loads = [
        pltpu.make_async_copy(src, dst, load_sem.at[i])
        for i, (src, dst) in enumerate(
            (
                (emb_hbm, emb_ref), (win_hbm, w_ref), (wq_hbm, wq_ref), (wk_hbm, wk_ref),
                (wv_hbm, wv_ref), (wo_hbm, wo_ref), (wkern_hbm, wkern_ref),
            )
        )
    ]
    for c in loads:
        c.start()

    pos = pos_ref[...].astype(F32)
    eye = iota((LANES, LANES), 0) == iota((LANES, LANES), 1)
    rank = jnp.zeros((1, ROWS), F32)
    for k in range(ROWS // LANES):
        part = pos[:, k * LANES : (k + 1) * LANES]
        col = jnp.sum(jnp.where(eye, part, 0.0), axis=1, keepdims=True)
        rank = rank + jnp.sum(jnp.where(col < pos, 1.0, 0.0), axis=0, keepdims=True)
    rank = rank.astype(I32)
    local = pos_ref[...] % ROWS
    slot = ((local % DIL) * GROUP + local // DIL).astype(F32)
    dest = iota((PEERS, ROWS), 0) * CAP
    lane = iota((PEERS, LANES), 1)
    table = jnp.zeros((PEERS, LANES), F32)
    for c in range(CAP):
        hit = jnp.where(dest + c == rank, slot, 0.0)
        table = jnp.where(lane == c, jnp.sum(hit, axis=1, keepdims=True), table)
    tab_ref[...] = table

    def spill(d, carry):
        ps_ref[d] = tab_ref[pl.ds(d, 1), :]
        return carry

    lax.fori_loop(0, PEERS, spill, 0)
    step = 256
    loads[0].wait()
    loads[1].wait()
    for k in range(ROWS // step):
        s_ref[pl.ds(k * step, step), :] = dot(
            emb_ref[pl.ds(k * step, step), :], w_ref[...]
        ).astype(BF16)
    for k in range(ROWS // step):
        pick = jnp.where(iota((step, ROWS), 0) + k * step == rank, 1.0, 0.0).astype(BF16)
        moved = dot(pick, s_ref[...]).reshape(step // CAP, CAP, D)
        both = jnp.concatenate([moved[:, :, :HALF], moved[:, :, HALF:]], axis=1)
        xs_ref[pl.ds(k * 2 * step, 2 * step), :] = both.reshape(2 * step, HALF).astype(BF16)

    mine_x = pltpu.make_async_copy(
        xs_ref.at[pl.ds(me * chunk, chunk), :], xr_ref.at[pl.ds(me * chunk, chunk), :], own.at[0]
    )
    mine_p = pltpu.make_async_copy(ps_ref.at[me], pr_ref.at[me], own.at[1])
    mine_x.start()
    mine_p.start()
    pl.semaphore_wait(barrier, PEERS - 1)

    def send(k, carry):
        peer = (me + k * SPREAD) % PEERS
        where = (peer // NREGION, peer % NREGION)
        pltpu.make_async_remote_copy(
            src_ref=ps_ref.at[peer], dst_ref=pr_ref.at[me],
            send_sem=sp, recv_sem=rp, device_id=where, device_id_type=MESH,
        ).start()
        pltpu.make_async_remote_copy(
            src_ref=xs_ref.at[pl.ds(peer * chunk, chunk), :],
            dst_ref=xr_ref.at[pl.ds(me * chunk, chunk), :],
            send_sem=sx, recv_sem=rx, device_id=where, device_id_type=MESH,
        ).start()
        return carry

    lax.fori_loop(1, PEERS, send, 0)

    for c in loads[2:]:
        c.wait()
    gap = jnp.zeros((D, LANES - 2 * HEAD), BF16)
    for src, dst in ((wq_ref, wq_out), (wk_ref, wk_out), (wv_ref, wv_out)):
        for j in range(PAIRS):
            pair = src[:, 2 * HEAD * j : 2 * HEAD * (j + 1)]
            dst[:, LANES * j : LANES * (j + 1)] = jnp.concatenate([pair, gap], axis=1)
    for j in range(PAIRS):
        wo_out[pl.ds(LANES * j, 2 * HEAD), :] = wo_ref[pl.ds(2 * HEAD * j, 2 * HEAD), :]
        wo_out[pl.ds(LANES * j + 2 * HEAD, LANES - 2 * HEAD), :] = jnp.zeros((LANES - 2 * HEAD, D), BF16)

    mine_x.wait()
    mine_p.wait()
    rest_x = pl.ds(0, (PEERS - 1) * chunk)
    rest_p = pl.ds(0, PEERS - 1)
    pltpu.make_async_copy(ps_ref.at[rest_p], pr_ref.at[rest_p], rp).wait()
    pltpu.make_async_copy(ps_ref.at[rest_p], pr_ref.at[rest_p], sp).wait()

    def fill(d, carry):
        tab_ref[pl.ds(d, 1), :] = pr_ref[d]
        return carry

    lax.fori_loop(0, PEERS, fill, 0)
    table = tab_ref[...]
    high = jnp.floor(table * (1.0 / 32.0))
    low = table - 32.0 * high
    spread = jnp.where(
        iota((LANES, ROWS), 0) == iota((LANES, ROWS), 1) % CAP, 1.0, 0.0
    ).astype(BF16)
    wide = 32.0 * dot(high.astype(BF16), spread) + dot(low.astype(BF16), spread)
    mine = iota((PEERS, ROWS), 0) == iota((PEERS, ROWS), 1) // CAP
    place = jnp.sum(jnp.where(mine, wide, 0.0), axis=0, keepdims=True).astype(I32)

    pltpu.make_async_copy(xs_ref.at[rest_x, :], xr_ref.at[rest_x, :], rx).wait()
    pltpu.make_async_copy(xs_ref.at[rest_x, :], xr_ref.at[rest_x, :], sx).wait()
    for k in range(ROWS // step):
        got = xr_ref[pl.ds(k * 2 * step, 2 * step), :].astype(F32)
        got = got.reshape(step // CAP, 2 * CAP, HALF)
        both = jnp.concatenate([got[:, :CAP, :], got[:, CAP:, :]], axis=2)
        s_ref[pl.ds(k * step, step), :] = both.reshape(step, D).astype(BF16)
    gain = gain_ref[...].astype(F32).reshape(1, D)
    for k in range(ROWS // step):
        pick = jnp.where(iota((step, ROWS), 0) + k * step == place, 1.0, 0.0).astype(BF16)
        rows = dot(pick, s_ref[...])
        start_ref[pl.ds(k * step, step), :] = rows.astype(BF16)
        center = rows - jnp.mean(rows, axis=1, keepdims=True)
        var = jnp.mean(center * center, axis=1, keepdims=True)
        normed_ref[pl.ds(k * step, step), :] = (center * lax.rsqrt(var + EPS) * gain).astype(BF16)

    enc, reg = lax.axis_index("enc"), lax.axis_index("region")
    after, before = (reg + 1) % NREGION, (reg + NREGION - 1) % NREGION
    edge = GROUP // 4
    near_copies, far_copies = [], []
    for kind, copies in ((0, near_copies), (1, far_copies)):
        for o in range(DIL):
            for way, dst, other in ((0, left_ref, after), (1, right_ref, before)):
                first = ((GROUP - edge, 0), (0, edge))[kind][way]
                rows = pl.ds(o * GROUP + first, (edge, GROUP - edge)[kind])
                copies.append(
                    pltpu.make_async_remote_copy(
                        src_ref=normed_ref.at[rows, :], dst_ref=dst.at[rows, :],
                        send_sem=send_sem.at[kind, way, o], recv_sem=recv_sem.at[kind, way, o],
                        device_id=(enc, other), device_id_type=MESH,
                    )
                )
    for c in near_copies:
        c.start()
    for c in far_copies:
        c.start()

    base = reg * ROWS
    near_ends = ends_of(near_ref[...])
    far_ends = ends_of(far_ref[...])
    near_cols, far_cols = pl.ds(0, PW), pl.ds(PW, PW)
    ones_lane = jnp.where(iota((GROUP, PW), 1) % LANES == 2 * HEAD, 1.0, 0.0)

    def tiled(marks):
        return jnp.concatenate([marks] * (PAIRS // 2), axis=1)

    def far_rows(o, b, ref):
        x = ref[pl.ds(o * GROUP, GROUP), :]
        seg = segment_of(base + (b - 1) * ROWS + DIL * iota((GROUP, 1), 0) + o, far_ends)
        dst = pl.ds(b * GROUP, GROUP)
        kf_ref[o, dst, :] = (dot(x, wk_out[:, far_cols]) + tiled(key_marks(seg))).astype(BF16)
        vf_ref[o, dst, :] = (dot(x, wv_out[:, far_cols]) + ones_lane).astype(BF16)
        return seg

    def near_rows(o, b, ref):
        first, count = ((GROUP - edge, edge), (0, GROUP), (0, edge))[b]
        x = ref[pl.ds(o * GROUP + first, count), :]
        pos = base + (b - 1) * ROWS + DIL * (iota((count, 1), 0) + first) + o
        seg = segment_of(pos, near_ends)
        dst = pl.ds((0, edge, edge + GROUP)[b], count)
        kn_ref[o, dst, :] = (dot(x, wk_out[:, near_cols]) + tiled(key_marks(seg))).astype(BF16)
        vn_ref[o, dst, :] = (dot(x, wv_out[:, near_cols]) + ones_lane[:count]).astype(BF16)
        return seg

    for o in range(DIL):
        rows = pl.ds(o * GROUP, GROUP)
        q_ref[rows, :] = dot(normed_ref[rows, :], wq_out[...]).astype(BF16)
        qm_ref[0, rows, :] = query_marks(near_rows(o, 1, normed_ref)).astype(BF16)
        qm_ref[1, rows, :] = query_marks(far_rows(o, 1, normed_ref)).astype(BF16)
    for c in near_copies:
        c.wait()
    for o in range(DIL):
        near_rows(o, 0, left_ref)
        near_rows(o, 2, right_ref)

    def near_block(b, carry):
        g = pl.multiple_of(b * 32, 32)

        def joined(ref, n, j):
            cols = slice(j * LANES, (j + 1) * LANES)
            return jnp.concatenate([ref[o, pl.ds(g, n), cols] for o in range(DIL)], axis=0)

        def query(j):
            cols = slice(j * LANES, (j + 1) * LANES)
            return jnp.concatenate(
                [q_ref[pl.ds(o * GROUP + g, 32), cols] for o in range(DIL)], axis=0
            )

        marks = jnp.concatenate(
            [qm_ref[0, pl.ds(o * GROUP + g, 32), :] for o in range(DIL)], axis=0
        )
        out = attend(query, marks, lambda j: joined(kn_ref, 160, j), lambda j: joined(vn_ref, 160, j))
        for o in range(DIL):
            ctx_ref[pl.ds(o * GROUP + g, 32), near_cols] = out[o * 32 : (o + 1) * 32, :]
        return carry

    lax.fori_loop(0, ROWS // 128, near_block, 0)
    for c in far_copies:
        c.wait()
    for o in range(DIL):
        far_rows(o, 0, left_ref)
        far_rows(o, 2, right_ref)

    def far_block(i, carry):
        o, half = i // 2, i % 2
        g = pl.multiple_of(half * 128, 128)
        rows = pl.ds(pl.multiple_of(o * GROUP + g, 128), 128)
        ctx_ref[rows, far_cols] = attend(
            lambda j: q_ref[rows, PW + j * LANES : PW + (j + 1) * LANES],
            qm_ref[1, rows, :],
            lambda j: kf_ref[o, pl.ds(g, 640), j * LANES : (j + 1) * LANES],
            lambda j: vf_ref[o, pl.ds(g, 640), j * LANES : (j + 1) * LANES],
        )
        return carry

    lax.fori_loop(0, ROWS // 128, far_block, 0)

    for o in range(DIL):
        rows = pl.ds(o * GROUP, GROUP)
        out = start_ref[rows, :].astype(F32) + dot(ctx_ref[rows, :], wo_out[...])
        s_ref[rows, :] = out.astype(BF16)
    step = 256
    for k in range(ROWS // step):
        r = iota((step, ROWS), 0) + k * step
        pick = jnp.where(
            iota((step, ROWS), 1) == (r % DIL) * GROUP + r // DIL, 1.0, 0.0
        ).astype(BF16)
        normed_ref[pl.ds(k * step, step), :] = dot(pick, s_ref[...]).astype(BF16)
    sel = jnp.where(
        iota((8, ROWS), 0) == iota((8, ROWS), 1) // REGION, tissue_ref[...], 0
    )
    pooled = dot(sel.astype(F32).astype(BF16), normed_ref[...]) / REGION
    store = pltpu.make_async_copy(normed_ref, feat_hbm, load_sem.at[7])
    store.start()

    core = reg % 2
    at = {"z": enc, "x": (reg // 2) % 4, "y": reg // 8}

    def device(shift):
        c = {a: (at[a] + shift.get(a, 0)) % 4 for a in AXES}
        return (c["z"], (c["y"] * 4 + c["x"]) * 2 + (core + shift.get("core", 0)) % 2)

    center = pooled - jnp.mean(pooled, axis=1, keepdims=True)
    var = jnp.mean(center * center, axis=1, keepdims=True)
    norm = center * lax.rsqrt(var + EPS)
    row = iota((8, D), 0)
    norm = jnp.where(row < 4, norm, 0.0)
    swapped = jnp.concatenate([norm[4:], norm[:4]], axis=0)
    pair_ref[0] = jnp.where(core == 0, norm, swapped)
    first = pltpu.make_async_remote_copy(
        src_ref=pair_ref.at[0], dst_ref=pair_ref.at[1], send_sem=ps, recv_sem=pr,
        device_id=device({"core": 1}), device_id_type=MESH,
    )
    first.start()
    first.wait()
    chip = pair_ref[0] + pair_ref[1]
    mine = jnp.where(core == 0, chip[:, :HALF], chip[:, HALF:])
    orders = [("z", "y", "x"), ("y", "x", "z"), ("x", "z", "y")]

    def offset(order):
        return ((at[order[2]] * 4 + at[order[1]]) * 4 + at[order[0]]) * 8

    for t, order in enumerate(orders):
        start = pl.multiple_of(offset(order), 8)
        half_ref[t, pl.ds(start, 8), :] = mine[:, t * LANES : (t + 1) * LANES]
    size = 8
    for stage in range(3):
        copies = []
        for t, order in enumerate(orders):
            start = pl.multiple_of(offset(order) // size * size, size)
            for k in (1, 2, 3):
                window = half_ref.at[t, pl.ds(start, size), :]
                copies.append(
                    pltpu.make_async_remote_copy(
                        src_ref=window, dst_ref=window,
                        send_sem=ss.at[stage, t, k - 1], recv_sem=rs.at[stage, t, k - 1],
                        device_id=device({order[stage]: k}), device_id_type=MESH,
                    )
                )
        for c in copies:
            c.start()
        for c in copies:
            c.wait()
        size *= 4
    last = pltpu.make_async_remote_copy(
        src_ref=half_ref, dst_ref=full_ref, send_sem=cs, recv_sem=cr,
        device_id=device({"core": 1}), device_id_type=MESH,
    )
    last.start()
    last.wait()

    for x in range(4):
        for y in range(4):
            for z in range(4):
                i = {"x": x, "y": y, "z": z}
                to = pl.ds(((x * 4 + y) * 4 + z) * 8, 8)
                for t, order in enumerate(orders):
                    src = pl.ds(((i[order[2]] * 4 + i[order[1]]) * 4 + i[order[0]]) * 8, 8)
                    a, b = half_ref[t, src, :], full_ref[t, src, :]
                    np_ref[to, t * LANES : (t + 1) * LANES] = jnp.where(core == 0, a, b)
                    np_ref[to, HALF + t * LANES : HALF + (t + 1) * LANES] = jnp.where(core == 0, b, a)

    n = PEERS * 4
    hp = lax.Precision.HIGHEST
    hosp = hosp_ref[...]
    ones = jnp.sum(hosp).astype(F32)
    per_slide = float(n // NENC)
    count_one = ones * per_slide
    count_zero = (NENC - ones) * per_slide

    def weights(slide, axis):
        label = jnp.zeros(slide.shape, I32)
        for s in range(NENC):
            label = jnp.where(slide == s, hosp[:, s : s + 1], label)
        return jnp.where(label == 1, 1.0 / count_one, -1.0 / count_zero)

    w_col = weights((iota((n, 1), 0) // 8) % 4, 0)
    w_row = weights((iota((1, n), 1) // 8) % 4, 1)
    normal = np_ref[...]
    emb = dot3(normal, wkern_ref[...])
    sq = emb * emb
    sq_col = jnp.sum(sq, axis=1, keepdims=True)
    sq_row = lax.dot_general(
        jnp.ones((8, sq.shape[1]), F32), sq, (((1,), (1,)), ((), ())), precision=hp,
        preferred_element_type=F32,
    )[0:1, :]
    inner = dot3(emb, emb, 1, 1)
    kern = jnp.exp(-(sq_col + sq_row - 2.0 * inner) / (2.0 * emb.shape[1])) * w_row
    sums = jnp.sum(kern, axis=1, keepdims=True)
    moments = dot3(kern, emb)
    stat = n * jnp.sum(w_col * sums)
    stat_ref[0, 0] = stat
    g = (-2.0 * n / emb.shape[1]) * w_col * (sums * emb - moments)
    grad_ref[...] = 100.0 * dot3(normal, g, 0, 0)
    store.wait()


def local(
    embeddings, tile_position, w_in, ln_gain, w_query, w_key, w_value, w_out,
    near_lengths, far_lengths, tissue, hospital, w_kernel,
):
    sds = jax.ShapeDtypeStruct
    dma, vmem = pltpu.SemaphoreType.DMA, pltpu.VMEM
    rows = vmem((ROWS, D), BF16)
    square = vmem((D, D), BF16)
    padded = vmem((D, PAIRS * LANES), BF16)
    features, stat, grad = pl.pallas_call(
        slide_kernel,
        out_shape=(sds((ROWS, D), BF16), sds((1, 1), F32), sds((D, 256), F32)),
        in_specs=[ANY, VM, ANY, VM, ANY, ANY, ANY, ANY, VM, VM, VM, VM, ANY],
        out_specs=(ANY, pl.BlockSpec(memory_space=pltpu.SMEM), VM),
        scratch_shapes=[
            vmem((ROWS, DIN), BF16), vmem((DIN, D), BF16), square, square, square, square,
            vmem((D, 256), F32), padded, padded, padded, vmem((PAIRS * LANES, D), BF16),
            rows, rows, rows,
            vmem((PEERS, LANES), F32),
            vmem((2 * ROWS, HALF), BF16), vmem((PEERS, 1, LANES), F32),
            vmem((2 * ROWS, HALF), BF16), vmem((PEERS, 1, LANES), F32),
            rows, rows,
            vmem((ROWS, 2 * PW), BF16), vmem((2, ROWS, LANES), BF16),
            vmem((DIL, GROUP + 128, PW), BF16), vmem((DIL, GROUP + 128, PW), BF16),
            vmem((DIL, 3 * GROUP, PW), BF16), vmem((DIL, 3 * GROUP, PW), BF16),
            vmem((ROWS, 2 * PW), BF16),
            vmem((2, 8, D), F32), vmem((3, 512, LANES), F32), vmem((3, 512, LANES), F32),
            vmem((512, D), F32),
            dma((8,)), dma, dma, dma, dma, dma((2,)), dma((2, 2, DIL)), dma((2, 2, DIL)),
            dma, dma, dma((3, 3, 3)), dma((3, 3, 3)), dma, dma,
        ],
        compiler_params=params(collective_id=0, has_side_effects=True),
        name="slide",
    )(
        embeddings, tile_position.reshape(1, ROWS), w_in, ln_gain, w_query, w_key, w_value, w_out,
        near_lengths, far_lengths, tissue.reshape(1, ROWS), hospital.reshape(1, NENC), w_kernel,
    )
    return features, stat.reshape(()), grad


def solution(mesh):
    split = P(("enc", "region"))
    return jax.shard_map(
        local,
        mesh=mesh,
        in_specs=(
            P(("enc", "region"), None), split, P(), P(), P(), P(), P(), P(), P(), P(), split, P(), P(),
        ),
        out_specs=(P(("enc", "region"), None), P(), P()),
        check_vma=False,
    )
```

```python
import functools

import jax
import jax.numpy as jnp
from jax import lax
from jax.experimental import pallas as pl
from jax.experimental.pallas import tpu as pltpu
from jax.sharding import PartitionSpec as P

MESH = pl.DeviceIdType.MESH
F32 = jnp.float32
BF16 = jnp.bfloat16
I32 = jnp.int32

ROWS = 1024
DIN = 1536
D = 768
PAIRS = 8
HEAD = 48
LANES = 128
PW = PAIRS // 2 * LANES
GROUP = 256
DIL = 4
REGION = 256
NENC = 4
NREGION = 32
PEERS = NENC * NREGION
CAP = 8
SEND_UNROLL = 1
SPREAD = 45
HALF = D // 2
EPS = 1e-05
BIG = 1e30
BITS = 9
PAD_SEG = 511
EXP_SCALE = 1.4426950408889634 / 48.0**0.5
VMEM_LIMIT = 60 * 1024 * 1024


def iota(shape, dim):
    return lax.broadcasted_iota(I32, shape, dim)


def dot(a, b):
    return jnp.dot(a, b, preferred_element_type=F32)


def params(**kw):
    return pltpu.CompilerParams(vmem_limit_bytes=VMEM_LIMIT, **kw)


VM = pl.BlockSpec(memory_space=pltpu.VMEM)
ANY = pl.BlockSpec(memory_space=pl.ANY)


def ends_of(lengths):
    n = lengths.shape[1]
    upto = jnp.where(iota((n, n), 0) <= iota((n, n), 1), 1.0, 0.0).astype(BF16)
    high, low = lengths // 32, lengths % 32
    sums = 32.0 * dot(high.astype(F32).astype(BF16), upto) + dot(low.astype(F32).astype(BF16), upto)
    own = iota(sums.shape, 0) == lax.axis_index("enc")
    return jnp.sum(jnp.where(own, sums, 0.0), axis=0, keepdims=True)


def segment_of(pos, ends):
    seg = jnp.sum(jnp.where(ends <= pos.astype(F32), 1.0, 0.0), axis=1, keepdims=True).astype(I32)
    return jnp.where((pos >= 0) & (pos < ROWS * NREGION), seg, PAD_SEG)


def key_marks(seg):
    lane = iota((seg.shape[0], LANES), 1) - 2 * HEAD
    bit = (seg >> jnp.where(lane >= BITS, lane - BITS, jnp.maximum(lane, 0)) % 16) & 1
    mark = jnp.where(lane < BITS, 1 - bit, bit)
    return jnp.where((lane >= 0) & (lane < 2 * BITS), mark, 0).astype(F32)


def query_marks(seg):
    lane = iota((seg.shape[0], LANES), 1) - 2 * HEAD
    bit = (seg >> jnp.where(lane >= BITS, lane - BITS, jnp.maximum(lane, 0)) % 16) & 1
    mark = jnp.where(lane < BITS, bit, 1 - bit)
    return jnp.where((lane >= 0) & (lane < 2 * BITS), mark, 0).astype(F32) * -BIG


def attend(query, marks, key, value):
    n = marks.shape[0]
    lane = iota((n, LANES), 1)
    pairs = range(PAIRS // 2)
    scores = []
    for j in pairs:
        both = query(j)
        q = jnp.concatenate(
            [
                jnp.where((lane >= h * HEAD) & (lane < (h + 1) * HEAD), both, marks)
                for h in range(2)
            ],
            axis=0,
        )
        scores.append(
            lax.dot_general(q, key(j), (((1,), (1,)), ((), ())), preferred_element_type=F32)
        )
    probs = [
        jnp.exp2((s - jnp.max(s, axis=1, keepdims=True)) * EXP_SCALE).astype(BF16) for s in scores
    ]
    out = []
    for j in pairs:
        o = dot(probs[j], value(j))
        o = o / o[:, 2 * HEAD : 2 * HEAD + 1]
        o = jnp.where(lane < HEAD, o[:n], jnp.where(lane < 2 * HEAD, o[n:], 0.0))
        out.append(o.astype(BF16))
    return jnp.concatenate(out, axis=1)


AXES = ("x", "y", "z")


def dot3(a, b, ca=1, cb=0):
    dims = (((ca,), (cb,)), ((), ()))

    def mul(x, y):
        return lax.dot_general(x, y, dims, preferred_element_type=F32)

    ah, bh = a.astype(BF16), b.astype(BF16)
    al, bl = (a - ah.astype(F32)).astype(BF16), (b - bh.astype(F32)).astype(BF16)
    return mul(ah, bh) + (mul(ah, bl) + mul(al, bh))


def slide_kernel(
    emb_hbm, pos_ref, win_hbm, gain_ref, wq_hbm, wk_hbm, wv_hbm, wo_hbm,
    near_ref, far_ref, tissue_ref, hosp_ref, wkern_hbm,
    feat_hbm, stat_ref, grad_ref,
    emb_ref, w_ref, wq_ref, wk_ref, wv_ref, wo_ref, wkern_ref, wq_out, wk_out, wv_out, wo_out,
    start_ref, normed_ref, s_ref, tab_ref, xs_ref, ps_ref, xr_ref, pr_ref,
    left_ref, right_ref, q_ref, qm_ref, kn_ref, vn_ref, kf_ref, vf_ref, ctx_ref,
    pair_ref, half_ref, full_ref, np_ref,
    load_sem, sx, rx, sp, rp, own, send_sem, recv_sem, pair_send, pair_recv, ss, rs, entered,
):
    enc, reg = lax.axis_index("enc"), lax.axis_index("region")
    me = enc * NREGION + reg
    core = reg % 2
    at = {"z": enc, "x": (reg // 2) % 4, "y": reg // 8}

    def device(shift):
        c = {a: (at[a] + shift.get(a, 0)) % 4 for a in AXES}
        return (c["z"], (c["y"] * 4 + c["x"]) * 2 + (core + shift.get("core", 0)) % 2)

    chunk = 2 * CAP
    barrier = pltpu.get_barrier_semaphore()

    plane_yz = [{"z": i, "y": j} for i in range(4) for j in range(4) if i or j]
    line_x = [{"x": i, "core": c} for i in range(4) for c in range(2) if i or c]
    for shift in plane_yz + line_x:
        pl.semaphore_signal(barrier, inc=1, device_id=device(shift), device_id_type=MESH)
    loads = [
        pltpu.make_async_copy(src, dst, load_sem.at[i])
        for i, (src, dst) in enumerate(
            (
                (emb_hbm, emb_ref), (win_hbm, w_ref), (wq_hbm, wq_ref), (wk_hbm, wk_ref),
                (wv_hbm, wv_ref), (wo_hbm, wo_ref), (wkern_hbm, wkern_ref),
            )
        )
    ]
    for c in loads:
        c.start()

    pos = pos_ref[...].astype(F32)
    eye = iota((LANES, LANES), 0) == iota((LANES, LANES), 1)
    rank = jnp.zeros((1, ROWS), F32)
    for k in range(ROWS // LANES):
        part = pos[:, k * LANES : (k + 1) * LANES]
        col = jnp.sum(jnp.where(eye, part, 0.0), axis=1, keepdims=True)
        rank = rank + jnp.sum(jnp.where(col < pos, 1.0, 0.0), axis=0, keepdims=True)
    rank = rank.astype(I32)
    local = pos_ref[...] % ROWS
    slot = ((local % DIL) * GROUP + local // DIL).astype(F32)
    dest = iota((PEERS, ROWS), 0) * CAP
    lane = iota((PEERS, LANES), 1)
    table = jnp.zeros((PEERS, LANES), F32)
    for c in range(CAP):
        hit = jnp.where(dest + c == rank, slot, 0.0)
        table = jnp.where(lane == c, jnp.sum(hit, axis=1, keepdims=True), table)
    tab_ref[...] = table

    def spill(d, carry):
        ps_ref[d] = tab_ref[pl.ds(d, 1), :]
        return carry

    lax.fori_loop(0, PEERS, spill, 0)
    step = 256
    loads[0].wait()
    loads[1].wait()
    for k in range(ROWS // step):
        s_ref[pl.ds(k * step, step), :] = dot(
            emb_ref[pl.ds(k * step, step), :], w_ref[...]
        ).astype(BF16)
    pl.semaphore_wait(barrier, len(plane_yz + line_x))
    for shift in line_x:
        pl.semaphore_signal(entered, inc=1, device_id=device(shift), device_id_type=MESH)
    for k in range(ROWS // step):
        pick = jnp.where(iota((step, ROWS), 0) + k * step == rank, 1.0, 0.0).astype(BF16)
        moved = dot(pick, s_ref[...]).reshape(step // CAP, CAP, D)
        both = jnp.concatenate([moved[:, :, :HALF], moved[:, :, HALF:]], axis=1)
        xs_ref[pl.ds(k * 2 * step, 2 * step), :] = both.reshape(2 * step, HALF).astype(BF16)

    mine_x = pltpu.make_async_copy(
        xs_ref.at[pl.ds(me * chunk, chunk), :], xr_ref.at[pl.ds(me * chunk, chunk), :], own.at[0]
    )
    mine_p = pltpu.make_async_copy(ps_ref.at[me], pr_ref.at[me], own.at[1])
    mine_x.start()
    mine_p.start()
    pl.semaphore_wait(entered, len(line_x))

    def send(k, carry):
        peer = (me + k * SPREAD) % PEERS
        pltpu.make_async_remote_copy(
            src_ref=ps_ref.at[peer], dst_ref=pr_ref.at[me],
            send_sem=sp, recv_sem=rp, device_id=peer, device_id_type=pl.DeviceIdType.LOGICAL,
        ).start()
        pltpu.make_async_remote_copy(
            src_ref=xs_ref.at[pl.ds(peer * chunk, chunk), :],
            dst_ref=xr_ref.at[pl.ds(me * chunk, chunk), :],
            send_sem=sx, recv_sem=rx, device_id=peer, device_id_type=pl.DeviceIdType.LOGICAL,
        ).start()
        return carry

    lax.fori_loop(1, PEERS, send, 0, unroll=SEND_UNROLL)

    for c in loads[2:]:
        c.wait()
    gap = jnp.zeros((D, LANES - 2 * HEAD), BF16)
    for src, dst in ((wq_ref, wq_out), (wk_ref, wk_out), (wv_ref, wv_out)):
        for j in range(PAIRS):
            pair = src[:, 2 * HEAD * j : 2 * HEAD * (j + 1)]
            dst[:, LANES * j : LANES * (j + 1)] = jnp.concatenate([pair, gap], axis=1)
    for j in range(PAIRS):
        wo_out[pl.ds(LANES * j, 2 * HEAD), :] = wo_ref[pl.ds(2 * HEAD * j, 2 * HEAD), :]
        wo_out[pl.ds(LANES * j + 2 * HEAD, LANES - 2 * HEAD), :] = jnp.zeros((LANES - 2 * HEAD, D), BF16)

    mine_x.wait()
    mine_p.wait()
    rest_x = pl.ds(0, (PEERS - 1) * chunk)
    rest_p = pl.ds(0, PEERS - 1)
    pltpu.make_async_copy(ps_ref.at[rest_p], pr_ref.at[rest_p], rp).wait()
    pltpu.make_async_copy(ps_ref.at[rest_p], pr_ref.at[rest_p], sp).wait()

    def fill(d, carry):
        tab_ref[pl.ds(d, 1), :] = pr_ref[d]
        return carry

    lax.fori_loop(0, PEERS, fill, 0)
    table = tab_ref[...]
    high = jnp.floor(table * (1.0 / 32.0))
    low = table - 32.0 * high
    spread = jnp.where(
        iota((LANES, ROWS), 0) == iota((LANES, ROWS), 1) % CAP, 1.0, 0.0
    ).astype(BF16)
    wide = 32.0 * dot(high.astype(BF16), spread) + dot(low.astype(BF16), spread)
    mine = iota((PEERS, ROWS), 0) == iota((PEERS, ROWS), 1) // CAP
    place = jnp.sum(jnp.where(mine, wide, 0.0), axis=0, keepdims=True).astype(I32)

    pltpu.make_async_copy(xs_ref.at[rest_x, :], xr_ref.at[rest_x, :], rx).wait()
    pltpu.make_async_copy(xs_ref.at[rest_x, :], xr_ref.at[rest_x, :], sx).wait()
    for k in range(ROWS // step):
        got = xr_ref[pl.ds(k * 2 * step, 2 * step), :].astype(F32)
        got = got.reshape(step // CAP, 2 * CAP, HALF)
        both = jnp.concatenate([got[:, :CAP, :], got[:, CAP:, :]], axis=2)
        s_ref[pl.ds(k * step, step), :] = both.reshape(step, D).astype(BF16)
    gain = gain_ref[...].astype(F32).reshape(1, D)
    for k in range(ROWS // step):
        pick = jnp.where(iota((step, ROWS), 0) + k * step == place, 1.0, 0.0).astype(BF16)
        rows = dot(pick, s_ref[...])
        start_ref[pl.ds(k * step, step), :] = rows.astype(BF16)
        center = rows - jnp.mean(rows, axis=1, keepdims=True)
        var = jnp.mean(center * center, axis=1, keepdims=True)
        normed_ref[pl.ds(k * step, step), :] = (center * lax.rsqrt(var + EPS) * gain).astype(BF16)

    after, before = (reg + 1) % NREGION, (reg + NREGION - 1) % NREGION
    edge = GROUP // 4
    near_copies, far_copies = [], []
    for kind, copies in ((0, near_copies), (1, far_copies)):
        for o in range(DIL):
            for way, dst, other in ((0, left_ref, after), (1, right_ref, before)):
                first = ((GROUP - edge, 0), (0, edge))[kind][way]
                rows = pl.ds(o * GROUP + first, (edge, GROUP - edge)[kind])
                copies.append(
                    pltpu.make_async_remote_copy(
                        src_ref=normed_ref.at[rows, :], dst_ref=dst.at[rows, :],
                        send_sem=send_sem.at[kind, way, o], recv_sem=recv_sem.at[kind, way, o],
                        device_id=(enc, other), device_id_type=MESH,
                    )
                )
    for c in near_copies:
        c.start()
    for c in far_copies:
        c.start()

    base = reg * ROWS
    near_ends = ends_of(near_ref[...])
    far_ends = ends_of(far_ref[...])
    near_cols, far_cols = pl.ds(0, PW), pl.ds(PW, PW)
    ones_lane = jnp.where(iota((GROUP, PW), 1) % LANES == 2 * HEAD, 1.0, 0.0)

    def tiled(marks):
        return jnp.concatenate([marks] * (PAIRS // 2), axis=1)

    def far_rows(o, b, ref):
        x = ref[pl.ds(o * GROUP, GROUP), :]
        seg = segment_of(base + (b - 1) * ROWS + DIL * iota((GROUP, 1), 0) + o, far_ends)
        dst = pl.ds(b * GROUP, GROUP)
        kf_ref[o, dst, :] = (dot(x, wk_out[:, far_cols]) + tiled(key_marks(seg))).astype(BF16)
        vf_ref[o, dst, :] = (dot(x, wv_out[:, far_cols]) + ones_lane).astype(BF16)
        return seg

    def near_rows(o, b, ref):
        first, count = ((GROUP - edge, edge), (0, GROUP), (0, edge))[b]
        x = ref[pl.ds(o * GROUP + first, count), :]
        pos = base + (b - 1) * ROWS + DIL * (iota((count, 1), 0) + first) + o
        seg = segment_of(pos, near_ends)
        dst = pl.ds((0, edge, edge + GROUP)[b], count)
        kn_ref[o, dst, :] = (dot(x, wk_out[:, near_cols]) + tiled(key_marks(seg))).astype(BF16)
        vn_ref[o, dst, :] = (dot(x, wv_out[:, near_cols]) + ones_lane[:count]).astype(BF16)
        return seg

    for o in range(DIL):
        rows = pl.ds(o * GROUP, GROUP)
        q_ref[rows, :] = dot(normed_ref[rows, :], wq_out[...]).astype(BF16)
        qm_ref[0, rows, :] = query_marks(near_rows(o, 1, normed_ref)).astype(BF16)
        qm_ref[1, rows, :] = query_marks(far_rows(o, 1, normed_ref)).astype(BF16)
    for c in near_copies:
        c.wait()
    for o in range(DIL):
        near_rows(o, 0, left_ref)
        near_rows(o, 2, right_ref)

    def near_block(b, carry):
        g = pl.multiple_of(b * 32, 32)

        def joined(ref, n, j):
            cols = slice(j * LANES, (j + 1) * LANES)
            return jnp.concatenate([ref[o, pl.ds(g, n), cols] for o in range(DIL)], axis=0)

        def query(j):
            cols = slice(j * LANES, (j + 1) * LANES)
            return jnp.concatenate(
                [q_ref[pl.ds(o * GROUP + g, 32), cols] for o in range(DIL)], axis=0
            )

        marks = jnp.concatenate(
            [qm_ref[0, pl.ds(o * GROUP + g, 32), :] for o in range(DIL)], axis=0
        )
        out = attend(query, marks, lambda j: joined(kn_ref, 160, j), lambda j: joined(vn_ref, 160, j))
        for o in range(DIL):
            ctx_ref[pl.ds(o * GROUP + g, 32), near_cols] = out[o * 32 : (o + 1) * 32, :]
        return carry

    lax.fori_loop(0, ROWS // 128, near_block, 0)
    for c in far_copies:
        c.wait()
    for o in range(DIL):
        far_rows(o, 0, left_ref)
        far_rows(o, 2, right_ref)

    def far_block(i, carry):
        o, half = i // 2, i % 2
        g = pl.multiple_of(half * 128, 128)
        rows = pl.ds(pl.multiple_of(o * GROUP + g, 128), 128)
        ctx_ref[rows, far_cols] = attend(
            lambda j: q_ref[rows, PW + j * LANES : PW + (j + 1) * LANES],
            qm_ref[1, rows, :],
            lambda j: kf_ref[o, pl.ds(g, 640), j * LANES : (j + 1) * LANES],
            lambda j: vf_ref[o, pl.ds(g, 640), j * LANES : (j + 1) * LANES],
        )
        return carry

    lax.fori_loop(0, ROWS // 128, far_block, 0)

    for o in range(DIL):
        rows = pl.ds(o * GROUP, GROUP)
        out = start_ref[rows, :].astype(F32) + dot(ctx_ref[rows, :], wo_out[...])
        s_ref[rows, :] = out.astype(BF16)
    step = 256
    for k in range(ROWS // step):
        r = iota((step, ROWS), 0) + k * step
        pick = jnp.where(
            iota((step, ROWS), 1) == (r % DIL) * GROUP + r // DIL, 1.0, 0.0
        ).astype(BF16)
        normed_ref[pl.ds(k * step, step), :] = dot(pick, s_ref[...]).astype(BF16)
    sel = jnp.where(
        iota((8, ROWS), 0) == iota((8, ROWS), 1) // REGION, tissue_ref[...], 0
    )
    pooled = dot(sel.astype(F32).astype(BF16), normed_ref[...]) / REGION
    store = pltpu.make_async_copy(normed_ref, feat_hbm, load_sem.at[7])
    store.start()

    center = pooled - jnp.mean(pooled, axis=1, keepdims=True)
    var = jnp.mean(center * center, axis=1, keepdims=True)
    norm = center * lax.rsqrt(var + EPS)
    row = iota((8, D), 0)
    norm = jnp.where(row < 4, norm, 0.0)
    swapped = jnp.concatenate([norm[4:], norm[:4]], axis=0)
    pair_ref[0] = jnp.where(core == 0, norm, swapped)
    first = pltpu.make_async_remote_copy(
        src_ref=pair_ref.at[0], dst_ref=pair_ref.at[1], send_sem=pair_send, recv_sem=pair_recv,
        device_id=device({"core": 1}), device_id_type=MESH,
    )
    first.start()
    first.wait()
    chip = pair_ref[0] + pair_ref[1]
    mine = jnp.where(core == 0, chip[:, :HALF], chip[:, HALF:])
    orders = [("z", "y", "x"), ("y", "x", "z"), ("x", "z", "y")]

    def offset(order):
        return ((at[order[2]] * 4 + at[order[1]]) * 4 + at[order[0]]) * 8

    for t, order in enumerate(orders):
        start = pl.multiple_of(offset(order), 8)
        half_ref[t, pl.ds(start, 8), :] = mine[:, t * LANES : (t + 1) * LANES]
    def plane(order):
        return [{order[0]: a, order[1]: b} for a in range(4) for b in range(4) if a or b]

    def remote(window, sems, peer):
        return pltpu.make_async_remote_copy(
            src_ref=window, dst_ref=window, send_sem=ss.at[sems], recv_sem=rs.at[sems],
            device_id=device(peer), device_id_type=MESH,
        )

    first, second, third = [], [], []
    for t, order in enumerate(orders):
        start = pl.multiple_of(offset(order), 8)
        window = half_ref.at[t, pl.ds(start, 8), :]
        first.append([remote(window, (t, i), p) for i, p in enumerate(plane(order))])
        window = half_ref.at[t, pl.ds(pl.multiple_of(start // 128 * 128, 128), 128), :]
        second.append([remote(window, (t, 15 + k), {order[2]: k + 1}) for k in range(3)])
        third.append(
            pltpu.make_async_remote_copy(
                src_ref=half_ref.at[t], dst_ref=full_ref.at[t],
                send_sem=ss.at[t, 18], recv_sem=rs.at[t, 18],
                device_id=device({"core": 1}), device_id_type=MESH,
            )
        )
    for copies in first:
        for c in copies:
            c.start()
    for t in range(3):
        for c in first[t]:
            c.wait()
        for c in second[t]:
            c.start()
    for t in range(3):
        for c in second[t]:
            c.wait()
        third[t].start()
    for t in range(3):
        third[t].wait()

    for x in range(4):
        for y in range(4):
            for z in range(4):
                i = {"x": x, "y": y, "z": z}
                to = pl.ds(((x * 4 + y) * 4 + z) * 8, 8)
                for t, order in enumerate(orders):
                    src = pl.ds(((i[order[2]] * 4 + i[order[1]]) * 4 + i[order[0]]) * 8, 8)
                    a, b = half_ref[t, src, :], full_ref[t, src, :]
                    np_ref[to, t * LANES : (t + 1) * LANES] = jnp.where(core == 0, a, b)
                    np_ref[to, HALF + t * LANES : HALF + (t + 1) * LANES] = jnp.where(core == 0, b, a)

    n = PEERS * 4
    hp = lax.Precision.HIGHEST
    hosp = hosp_ref[...]
    ones = jnp.sum(hosp).astype(F32)
    per_slide = float(n // NENC)
    count_one = ones * per_slide
    count_zero = (NENC - ones) * per_slide

    def weights(slide, axis):
        label = jnp.zeros(slide.shape, I32)
        for s in range(NENC):
            label = jnp.where(slide == s, hosp[:, s : s + 1], label)
        return jnp.where(label == 1, 1.0 / count_one, -1.0 / count_zero)

    w_col = weights((iota((n, 1), 0) // 8) % 4, 0)
    w_row = weights((iota((1, n), 1) // 8) % 4, 1)
    normal = np_ref[...]
    emb = dot3(normal, wkern_ref[...])
    sq = emb * emb
    sq_col = jnp.sum(sq, axis=1, keepdims=True)
    sq_row = lax.dot_general(
        jnp.ones((8, sq.shape[1]), F32), sq, (((1,), (1,)), ((), ())), precision=hp,
        preferred_element_type=F32,
    )[0:1, :]
    inner = dot3(emb, emb, 1, 1)
    kern = jnp.exp(-(sq_col + sq_row - 2.0 * inner) / (2.0 * emb.shape[1])) * w_row
    sums = jnp.sum(kern, axis=1, keepdims=True)
    moments = dot3(kern, emb)
    stat = n * jnp.sum(w_col * sums)
    stat_ref[0, 0] = stat
    g = (-2.0 * n / emb.shape[1]) * w_col * (sums * emb - moments)
    grad_ref[...] = 100.0 * dot3(normal, g, 0, 0)
    store.wait()


def local(
    embeddings, tile_position, w_in, ln_gain, w_query, w_key, w_value, w_out,
    near_lengths, far_lengths, tissue, hospital, w_kernel,
):
    sds = jax.ShapeDtypeStruct
    dma, vmem = pltpu.SemaphoreType.DMA, pltpu.VMEM
    rows = vmem((ROWS, D), BF16)
    square = vmem((D, D), BF16)
    padded = vmem((D, PAIRS * LANES), BF16)
    features, stat, grad = pl.pallas_call(
        slide_kernel,
        out_shape=(sds((ROWS, D), BF16), sds((1, 1), F32), sds((D, 256), F32)),
        in_specs=[ANY, VM, ANY, VM, ANY, ANY, ANY, ANY, VM, VM, VM, VM, ANY],
        out_specs=(ANY, pl.BlockSpec(memory_space=pltpu.SMEM), VM),
        scratch_shapes=[
            vmem((ROWS, DIN), BF16), vmem((DIN, D), BF16), square, square, square, square,
            vmem((D, 256), F32), padded, padded, padded, vmem((PAIRS * LANES, D), BF16),
            rows, rows, rows,
            vmem((PEERS, LANES), F32),
            vmem((2 * ROWS, HALF), BF16), vmem((PEERS, 1, LANES), F32),
            vmem((2 * ROWS, HALF), BF16), vmem((PEERS, 1, LANES), F32),
            rows, rows,
            vmem((ROWS, 2 * PW), BF16), vmem((2, ROWS, LANES), BF16),
            vmem((DIL, GROUP + 128, PW), BF16), vmem((DIL, GROUP + 128, PW), BF16),
            vmem((DIL, 3 * GROUP, PW), BF16), vmem((DIL, 3 * GROUP, PW), BF16),
            vmem((ROWS, 2 * PW), BF16),
            vmem((2, 8, D), F32), vmem((3, 512, LANES), F32), vmem((3, 512, LANES), F32),
            vmem((512, D), F32),
            dma((8,)), dma, dma, dma, dma, dma((2,)), dma((2, 2, DIL)), dma((2, 2, DIL)),
            dma, dma, dma((3, 19)), dma((3, 19)), pltpu.SemaphoreType.REGULAR,
        ],
        compiler_params=params(collective_id=0, has_side_effects=True),
        name="slide",
    )(
        embeddings, tile_position.reshape(1, ROWS), w_in, ln_gain, w_query, w_key, w_value, w_out,
        near_lengths, far_lengths, tissue.reshape(1, ROWS), hospital.reshape(1, NENC), w_kernel,
    )
    return features, stat.reshape(()), grad


def solution(mesh):
    split = P(("enc", "region"))
    return jax.shard_map(
        local,
        mesh=mesh,
        in_specs=(
            P(("enc", "region"), None), split, P(), P(), P(), P(), P(), P(), P(), P(), split, P(), P(),
        ),
        out_specs=(P(("enc", "region"), None), P(), P()),
        check_vma=False,
    )
```

```python
import functools

import jax
import jax.numpy as jnp
from jax import lax
from jax.experimental import pallas as pl
from jax.experimental.pallas import tpu as pltpu
from jax.sharding import PartitionSpec as P

MESH = pl.DeviceIdType.MESH
F32 = jnp.float32
BF16 = jnp.bfloat16
I32 = jnp.int32

ROWS = 1024
DIN = 1536
D = 768
PAIRS = 8
HEAD = 48
LANES = 128
PW = PAIRS // 2 * LANES
GROUP = 256
DIL = 4
REGION = 256
NENC = 4
NREGION = 32
PEERS = NENC * NREGION
CAP = 8
SEND_UNROLL = 1
SPREAD = 45
HALF = D // 2
EPS = 1e-05
BIG = 1e30
BITS = 9
PAD_SEG = 511
EXP_SCALE = 1.4426950408889634 / 48.0**0.5
VMEM_LIMIT = 60 * 1024 * 1024


def iota(shape, dim):
    return lax.broadcasted_iota(I32, shape, dim)


def dot(a, b):
    return jnp.dot(a, b, preferred_element_type=F32)


def params(**kw):
    return pltpu.CompilerParams(vmem_limit_bytes=VMEM_LIMIT, **kw)


VM = pl.BlockSpec(memory_space=pltpu.VMEM)
ANY = pl.BlockSpec(memory_space=pl.ANY)


def ends_of(lengths):
    n = lengths.shape[1]
    upto = jnp.where(iota((n, n), 0) <= iota((n, n), 1), 1.0, 0.0).astype(BF16)
    high, low = lengths // 32, lengths % 32
    sums = 32.0 * dot(high.astype(F32).astype(BF16), upto) + dot(low.astype(F32).astype(BF16), upto)
    own = iota(sums.shape, 0) == lax.axis_index("enc")
    return jnp.sum(jnp.where(own, sums, 0.0), axis=0, keepdims=True)


def segment_of(pos, ends):
    seg = jnp.sum(jnp.where(ends <= pos.astype(F32), 1.0, 0.0), axis=1, keepdims=True).astype(I32)
    return jnp.where((pos >= 0) & (pos < ROWS * NREGION), seg, PAD_SEG)


def key_marks(seg):
    lane = iota((seg.shape[0], LANES), 1) - 2 * HEAD
    bit = (seg >> jnp.where(lane >= BITS, lane - BITS, jnp.maximum(lane, 0)) % 16) & 1
    mark = jnp.where(lane < BITS, 1 - bit, bit)
    return jnp.where((lane >= 0) & (lane < 2 * BITS), mark, 0).astype(F32)


def query_marks(seg):
    lane = iota((seg.shape[0], LANES), 1) - 2 * HEAD
    bit = (seg >> jnp.where(lane >= BITS, lane - BITS, jnp.maximum(lane, 0)) % 16) & 1
    mark = jnp.where(lane < BITS, bit, 1 - bit)
    return jnp.where((lane >= 0) & (lane < 2 * BITS), mark, 0).astype(F32) * -BIG


def attend(query, marks, key, value):
    n = marks.shape[0]
    lane = iota((n, LANES), 1)
    pairs = range(PAIRS // 2)
    scores = []
    for j in pairs:
        both = query(j)
        q = jnp.concatenate(
            [
                jnp.where((lane >= h * HEAD) & (lane < (h + 1) * HEAD), both, marks)
                for h in range(2)
            ],
            axis=0,
        )
        scores.append(
            lax.dot_general(q, key(j), (((1,), (1,)), ((), ())), preferred_element_type=F32)
        )
    probs = [
        jnp.exp2((s - jnp.max(s, axis=1, keepdims=True)) * EXP_SCALE).astype(BF16) for s in scores
    ]
    out = []
    for j in pairs:
        o = dot(probs[j], value(j))
        o = o / o[:, 2 * HEAD : 2 * HEAD + 1]
        o = jnp.where(lane < HEAD, o[:n], jnp.where(lane < 2 * HEAD, o[n:], 0.0))
        out.append(o.astype(BF16))
    return jnp.concatenate(out, axis=1)


AXES = ("x", "y", "z")


def dot3(a, b, ca=1, cb=0):
    dims = (((ca,), (cb,)), ((), ()))

    def mul(x, y):
        return lax.dot_general(x, y, dims, preferred_element_type=F32)

    ah, bh = a.astype(BF16), b.astype(BF16)
    al, bl = (a - ah.astype(F32)).astype(BF16), (b - bh.astype(F32)).astype(BF16)
    return mul(ah, bh) + (mul(ah, bl) + mul(al, bh))


def slide_kernel(
    emb_hbm, pos_ref, win_hbm, gain_ref, wq_hbm, wk_hbm, wv_hbm, wo_hbm,
    near_ref, far_ref, tissue_ref, hosp_ref, wkern_hbm,
    feat_hbm, stat_ref, grad_ref,
    emb_ref, w_ref, wq_ref, wk_ref, wv_ref, wo_ref, wkern_ref, wq_out, wk_out, wv_out, wo_out,
    start_ref, normed_ref, s_ref, tab_ref, xs_ref, ps_ref, xr_ref, pr_ref,
    sel_ref, left_ref, right_ref, q_ref, qm_ref, kn_ref, vn_ref, kf_ref, vf_ref, ctx_ref,
    pair_ref, half_ref, full_ref, np_ref,
    load_sem, sx, rx, sp, rp, own, send_sem, recv_sem, pair_send, pair_recv, ss, rs, entered,
):
    enc, reg = lax.axis_index("enc"), lax.axis_index("region")
    me = enc * NREGION + reg
    core = reg % 2
    at = {"z": enc, "x": (reg // 2) % 4, "y": reg // 8}

    def device(shift):
        c = {a: (at[a] + shift.get(a, 0)) % 4 for a in AXES}
        return (c["z"], (c["y"] * 4 + c["x"]) * 2 + (core + shift.get("core", 0)) % 2)

    chunk = 2 * CAP
    barrier = pltpu.get_barrier_semaphore()

    plane_yz = [{"z": i, "y": j} for i in range(4) for j in range(4) if i or j]
    line_x = [{"x": i, "core": c} for i in range(4) for c in range(2) if i or c]
    for shift in plane_yz + line_x:
        pl.semaphore_signal(barrier, inc=1, device_id=device(shift), device_id_type=MESH)
    loads = [
        pltpu.make_async_copy(src, dst, load_sem.at[i])
        for i, (src, dst) in enumerate(
            (
                (emb_hbm, emb_ref), (win_hbm, w_ref), (wq_hbm, wq_ref), (wk_hbm, wk_ref),
                (wv_hbm, wv_ref), (wo_hbm, wo_ref), (wkern_hbm, wkern_ref),
            )
        )
    ]
    for c in loads:
        c.start()

    pos = pos_ref[...].astype(F32)
    eye = iota((LANES, LANES), 0) == iota((LANES, LANES), 1)
    rank = jnp.zeros((1, ROWS), F32)
    for k in range(ROWS // LANES):
        part = pos[:, k * LANES : (k + 1) * LANES]
        col = jnp.sum(jnp.where(eye, part, 0.0), axis=1, keepdims=True)
        rank = rank + jnp.sum(jnp.where(col < pos, 1.0, 0.0), axis=0, keepdims=True)
    rank = rank.astype(I32)
    local = pos_ref[...] % ROWS
    slot = ((local % DIL) * GROUP + local // DIL).astype(F32)
    dest = iota((PEERS, ROWS), 0) * CAP
    lane = iota((PEERS, LANES), 1)
    table = jnp.zeros((PEERS, LANES), F32)
    for c in range(CAP):
        hit = jnp.where(dest + c == rank, slot, 0.0)
        table = jnp.where(lane == c, jnp.sum(hit, axis=1, keepdims=True), table)
    tab_ref[...] = table

    def spill(d, carry):
        ps_ref[d] = tab_ref[pl.ds(d, 1), :]
        return carry

    lax.fori_loop(0, PEERS, spill, 0)
    step = 256
    loads[0].wait()
    loads[1].wait()
    for k in range(ROWS // step):
        s_ref[pl.ds(k * step, step), :] = dot(
            emb_ref[pl.ds(k * step, step), :], w_ref[...]
        ).astype(BF16)
    pl.semaphore_wait(barrier, len(plane_yz + line_x))
    for shift in line_x:
        pl.semaphore_signal(entered, inc=1, device_id=device(shift), device_id_type=MESH)
    for k in range(ROWS // step):
        pick = jnp.where(iota((step, ROWS), 0) + k * step == rank, 1.0, 0.0).astype(BF16)
        moved = dot(pick, s_ref[...]).reshape(step // CAP, CAP, D)
        both = jnp.concatenate([moved[:, :, :HALF], moved[:, :, HALF:]], axis=1)
        xs_ref[pl.ds(k * 2 * step, 2 * step), :] = both.reshape(2 * step, HALF).astype(BF16)

    mine_x = pltpu.make_async_copy(
        xs_ref.at[pl.ds(me * chunk, chunk), :], xr_ref.at[pl.ds(me * chunk, chunk), :], own.at[0]
    )
    mine_p = pltpu.make_async_copy(ps_ref.at[me], pr_ref.at[me], own.at[1])
    mine_x.start()
    mine_p.start()
    pl.semaphore_wait(entered, len(line_x))

    def send(k, carry):
        peer = (me + k * SPREAD) % PEERS
        pltpu.make_async_remote_copy(
            src_ref=ps_ref.at[peer], dst_ref=pr_ref.at[me],
            send_sem=sp, recv_sem=rp, device_id=peer, device_id_type=pl.DeviceIdType.LOGICAL,
        ).start()
        pltpu.make_async_remote_copy(
            src_ref=xs_ref.at[pl.ds(peer * chunk, chunk), :],
            dst_ref=xr_ref.at[pl.ds(me * chunk, chunk), :],
            send_sem=sx, recv_sem=rx, device_id=peer, device_id_type=pl.DeviceIdType.LOGICAL,
        ).start()
        return carry

    lax.fori_loop(1, PEERS, send, 0, unroll=SEND_UNROLL)

    for c in loads[2:]:
        c.wait()
    gap = jnp.zeros((D, LANES - 2 * HEAD), BF16)
    for src, dst in ((wq_ref, wq_out), (wk_ref, wk_out), (wv_ref, wv_out)):
        for j in range(PAIRS):
            pair = src[:, 2 * HEAD * j : 2 * HEAD * (j + 1)]
            dst[:, LANES * j : LANES * (j + 1)] = jnp.concatenate([pair, gap], axis=1)
    for j in range(PAIRS):
        wo_out[pl.ds(LANES * j, 2 * HEAD), :] = wo_ref[pl.ds(2 * HEAD * j, 2 * HEAD), :]
        wo_out[pl.ds(LANES * j + 2 * HEAD, LANES - 2 * HEAD), :] = jnp.zeros((LANES - 2 * HEAD, D), BF16)

    chosen = jnp.where(
        iota((8, ROWS), 0) == iota((8, ROWS), 1) // REGION, tissue_ref[...], 0
    ).astype(F32).astype(BF16)
    for o in range(DIL):
        moves = iota((ROWS, GROUP), 0) == iota((ROWS, GROUP), 1) * DIL + o
        sel_ref[:, o * GROUP : (o + 1) * GROUP] = dot(chosen, jnp.where(moves, 1.0, 0.0).astype(BF16))

    mine_x.wait()
    mine_p.wait()
    rest_x = pl.ds(0, (PEERS - 1) * chunk)
    rest_p = pl.ds(0, PEERS - 1)
    pltpu.make_async_copy(ps_ref.at[rest_p], pr_ref.at[rest_p], rp).wait()
    pltpu.make_async_copy(ps_ref.at[rest_p], pr_ref.at[rest_p], sp).wait()

    def fill(d, carry):
        tab_ref[pl.ds(d, 1), :] = pr_ref[d]
        return carry

    lax.fori_loop(0, PEERS, fill, 0)
    table = tab_ref[...]
    high = jnp.floor(table * (1.0 / 32.0))
    low = table - 32.0 * high
    spread = jnp.where(
        iota((LANES, ROWS), 0) == iota((LANES, ROWS), 1) % CAP, 1.0, 0.0
    ).astype(BF16)
    wide = 32.0 * dot(high.astype(BF16), spread) + dot(low.astype(BF16), spread)
    mine = iota((PEERS, ROWS), 0) == iota((PEERS, ROWS), 1) // CAP
    place = jnp.sum(jnp.where(mine, wide, 0.0), axis=0, keepdims=True).astype(I32)

    pltpu.make_async_copy(xs_ref.at[rest_x, :], xr_ref.at[rest_x, :], rx).wait()
    pltpu.make_async_copy(xs_ref.at[rest_x, :], xr_ref.at[rest_x, :], sx).wait()
    for k in range(ROWS // step):
        got = xr_ref[pl.ds(k * 2 * step, 2 * step), :].astype(F32)
        got = got.reshape(step // CAP, 2 * CAP, HALF)
        both = jnp.concatenate([got[:, :CAP, :], got[:, CAP:, :]], axis=2)
        s_ref[pl.ds(k * step, step), :] = both.reshape(step, D).astype(BF16)
    gain = gain_ref[...].astype(F32).reshape(1, D)
    for k in range(ROWS // step):
        pick = jnp.where(iota((step, ROWS), 0) + k * step == place, 1.0, 0.0).astype(BF16)
        rows = dot(pick, s_ref[...])
        start_ref[pl.ds(k * step, step), :] = rows.astype(BF16)
        center = rows - jnp.mean(rows, axis=1, keepdims=True)
        var = jnp.mean(center * center, axis=1, keepdims=True)
        normed_ref[pl.ds(k * step, step), :] = (center * lax.rsqrt(var + EPS) * gain).astype(BF16)

    after, before = (reg + 1) % NREGION, (reg + NREGION - 1) % NREGION
    edge = GROUP // 4
    near_copies, far_copies = [], []
    for kind, copies in ((0, near_copies), (1, far_copies)):
        for o in range(DIL):
            for way, dst, other in ((0, left_ref, after), (1, right_ref, before)):
                first = ((GROUP - edge, 0), (0, edge))[kind][way]
                rows = pl.ds(o * GROUP + first, (edge, GROUP - edge)[kind])
                copies.append(
                    pltpu.make_async_remote_copy(
                        src_ref=normed_ref.at[rows, :], dst_ref=dst.at[rows, :],
                        send_sem=send_sem.at[kind, way, o], recv_sem=recv_sem.at[kind, way, o],
                        device_id=(enc, other), device_id_type=MESH,
                    )
                )
    for c in near_copies:
        c.start()
    for c in far_copies:
        c.start()

    base = reg * ROWS
    near_ends = ends_of(near_ref[...])
    far_ends = ends_of(far_ref[...])
    near_cols, far_cols = pl.ds(0, PW), pl.ds(PW, PW)
    ones_lane = jnp.where(iota((GROUP, PW), 1) % LANES == 2 * HEAD, 1.0, 0.0)

    def tiled(marks):
        return jnp.concatenate([marks] * (PAIRS // 2), axis=1)

    def far_rows(o, b, ref):
        x = ref[pl.ds(o * GROUP, GROUP), :]
        seg = segment_of(base + (b - 1) * ROWS + DIL * iota((GROUP, 1), 0) + o, far_ends)
        dst = pl.ds(b * GROUP, GROUP)
        kf_ref[o, dst, :] = (dot(x, wk_out[:, far_cols]) + tiled(key_marks(seg))).astype(BF16)
        vf_ref[o, dst, :] = (dot(x, wv_out[:, far_cols]) + ones_lane).astype(BF16)
        return seg

    def near_rows(o, b, ref):
        first, count = ((GROUP - edge, edge), (0, GROUP), (0, edge))[b]
        x = ref[pl.ds(o * GROUP + first, count), :]
        pos = base + (b - 1) * ROWS + DIL * (iota((count, 1), 0) + first) + o
        seg = segment_of(pos, near_ends)
        dst = pl.ds((0, edge, edge + GROUP)[b], count)
        kn_ref[o, dst, :] = (dot(x, wk_out[:, near_cols]) + tiled(key_marks(seg))).astype(BF16)
        vn_ref[o, dst, :] = (dot(x, wv_out[:, near_cols]) + ones_lane[:count]).astype(BF16)
        return seg

    for o in range(DIL):
        rows = pl.ds(o * GROUP, GROUP)
        q_ref[rows, :] = dot(normed_ref[rows, :], wq_out[...]).astype(BF16)
        qm_ref[0, rows, :] = query_marks(near_rows(o, 1, normed_ref)).astype(BF16)
        qm_ref[1, rows, :] = query_marks(far_rows(o, 1, normed_ref)).astype(BF16)
    for c in near_copies:
        c.wait()
    for o in range(DIL):
        near_rows(o, 0, left_ref)
        near_rows(o, 2, right_ref)

    def near_block(b, carry):
        g = pl.multiple_of(b * 32, 32)

        def joined(ref, n, j):
            cols = slice(j * LANES, (j + 1) * LANES)
            return jnp.concatenate([ref[o, pl.ds(g, n), cols] for o in range(DIL)], axis=0)

        def query(j):
            cols = slice(j * LANES, (j + 1) * LANES)
            return jnp.concatenate(
                [q_ref[pl.ds(o * GROUP + g, 32), cols] for o in range(DIL)], axis=0
            )

        marks = jnp.concatenate(
            [qm_ref[0, pl.ds(o * GROUP + g, 32), :] for o in range(DIL)], axis=0
        )
        out = attend(query, marks, lambda j: joined(kn_ref, 160, j), lambda j: joined(vn_ref, 160, j))
        for o in range(DIL):
            ctx_ref[pl.ds(o * GROUP + g, 32), near_cols] = out[o * 32 : (o + 1) * 32, :]
        return carry

    lax.fori_loop(0, ROWS // 128, near_block, 0)
    for c in far_copies:
        c.wait()
    for o in range(DIL):
        far_rows(o, 0, left_ref)
        far_rows(o, 2, right_ref)

    def far_block(i, carry):
        o, half = i // 2, i % 2
        g = pl.multiple_of(half * 128, 128)
        rows = pl.ds(pl.multiple_of(o * GROUP + g, 128), 128)
        ctx_ref[rows, far_cols] = attend(
            lambda j: q_ref[rows, PW + j * LANES : PW + (j + 1) * LANES],
            qm_ref[1, rows, :],
            lambda j: kf_ref[o, pl.ds(g, 640), j * LANES : (j + 1) * LANES],
            lambda j: vf_ref[o, pl.ds(g, 640), j * LANES : (j + 1) * LANES],
        )
        return carry

    lax.fori_loop(0, ROWS // 128, far_block, 0)

    for o in range(DIL):
        rows = pl.ds(o * GROUP, GROUP)
        out = start_ref[rows, :].astype(F32) + dot(ctx_ref[rows, :], wo_out[...])
        s_ref[rows, :] = out.astype(BF16)
    pooled = dot(sel_ref[...].astype(BF16), s_ref[...]) / REGION

    def reorder(k):
        r = iota((step, ROWS), 0) + k * step
        pick = jnp.where(
            iota((step, ROWS), 1) == (r % DIL) * GROUP + r // DIL, 1.0, 0.0
        ).astype(BF16)
        normed_ref[pl.ds(k * step, step), :] = dot(pick, s_ref[...]).astype(BF16)

    center = pooled - jnp.mean(pooled, axis=1, keepdims=True)
    var = jnp.mean(center * center, axis=1, keepdims=True)
    norm = center * lax.rsqrt(var + EPS)
    row = iota((8, D), 0)
    norm = jnp.where(row < 4, norm, 0.0)
    swapped = jnp.concatenate([norm[4:], norm[:4]], axis=0)
    pair_ref[0] = jnp.where(core == 0, norm, swapped)
    first = pltpu.make_async_remote_copy(
        src_ref=pair_ref.at[0], dst_ref=pair_ref.at[1], send_sem=pair_send, recv_sem=pair_recv,
        device_id=device({"core": 1}), device_id_type=MESH,
    )
    first.start()
    reorder(0)
    first.wait()
    chip = pair_ref[0] + pair_ref[1]
    mine = jnp.where(core == 0, chip[:, :HALF], chip[:, HALF:])
    orders = [("z", "y", "x"), ("y", "x", "z"), ("x", "z", "y")]

    def offset(order):
        return ((at[order[2]] * 4 + at[order[1]]) * 4 + at[order[0]]) * 8

    for t, order in enumerate(orders):
        start = pl.multiple_of(offset(order), 8)
        half_ref[t, pl.ds(start, 8), :] = mine[:, t * LANES : (t + 1) * LANES]
    def plane(order):
        return [{order[0]: a, order[1]: b} for a in range(4) for b in range(4) if a or b]

    def remote(window, sems, peer):
        return pltpu.make_async_remote_copy(
            src_ref=window, dst_ref=window, send_sem=ss.at[sems], recv_sem=rs.at[sems],
            device_id=device(peer), device_id_type=MESH,
        )

    first, second, third = [], [], []
    for t, order in enumerate(orders):
        start = pl.multiple_of(offset(order), 8)
        window = half_ref.at[t, pl.ds(start, 8), :]
        first.append([remote(window, (t, i), p) for i, p in enumerate(plane(order))])
        window = half_ref.at[t, pl.ds(pl.multiple_of(start // 128 * 128, 128), 128), :]
        second.append([remote(window, (t, 15 + k), {order[2]: k + 1}) for k in range(3)])
        third.append(
            pltpu.make_async_remote_copy(
                src_ref=half_ref.at[t], dst_ref=full_ref.at[t],
                send_sem=ss.at[t, 18], recv_sem=rs.at[t, 18],
                device_id=device({"core": 1}), device_id_type=MESH,
            )
        )
    for copies in first:
        for c in copies:
            c.start()
    for k in range(1, ROWS // step):
        reorder(k)
    store = pltpu.make_async_copy(normed_ref, feat_hbm, load_sem.at[7])
    store.start()
    for t in range(3):
        for c in first[t]:
            c.wait()
        for c in second[t]:
            c.start()
    for t in range(3):
        for c in second[t]:
            c.wait()
        third[t].start()
    for t in range(3):
        third[t].wait()

    for x in range(4):
        for y in range(4):
            for z in range(4):
                i = {"x": x, "y": y, "z": z}
                to = pl.ds(((x * 4 + y) * 4 + z) * 8, 8)
                for t, order in enumerate(orders):
                    src = pl.ds(((i[order[2]] * 4 + i[order[1]]) * 4 + i[order[0]]) * 8, 8)
                    a, b = half_ref[t, src, :], full_ref[t, src, :]
                    np_ref[to, t * LANES : (t + 1) * LANES] = jnp.where(core == 0, a, b)
                    np_ref[to, HALF + t * LANES : HALF + (t + 1) * LANES] = jnp.where(core == 0, b, a)

    n = PEERS * 4
    hp = lax.Precision.HIGHEST
    hosp = hosp_ref[...]
    ones = jnp.sum(hosp).astype(F32)
    per_slide = float(n // NENC)
    count_one = ones * per_slide
    count_zero = (NENC - ones) * per_slide

    def weights(slide, axis):
        label = jnp.zeros(slide.shape, I32)
        for s in range(NENC):
            label = jnp.where(slide == s, hosp[:, s : s + 1], label)
        return jnp.where(label == 1, 1.0 / count_one, -1.0 / count_zero)

    w_col = weights((iota((n, 1), 0) // 8) % 4, 0)
    w_row = weights((iota((1, n), 1) // 8) % 4, 1)
    normal = np_ref[...]
    emb = dot3(normal, wkern_ref[...])
    sq = emb * emb
    sq_col = jnp.sum(sq, axis=1, keepdims=True)
    sq_row = lax.dot_general(
        jnp.ones((8, sq.shape[1]), F32), sq, (((1,), (1,)), ((), ())), precision=hp,
        preferred_element_type=F32,
    )[0:1, :]
    inner = dot3(emb, emb, 1, 1)
    kern = jnp.exp(-(sq_col + sq_row - 2.0 * inner) / (2.0 * emb.shape[1])) * w_row
    sums = jnp.sum(kern, axis=1, keepdims=True)
    moments = dot3(kern, emb)
    stat = n * jnp.sum(w_col * sums)
    stat_ref[0, 0] = stat
    g = (-2.0 * n / emb.shape[1]) * w_col * (sums * emb - moments)
    grad_ref[...] = 100.0 * dot3(normal, g, 0, 0)
    store.wait()


def local(
    embeddings, tile_position, w_in, ln_gain, w_query, w_key, w_value, w_out,
    near_lengths, far_lengths, tissue, hospital, w_kernel,
):
    sds = jax.ShapeDtypeStruct
    dma, vmem = pltpu.SemaphoreType.DMA, pltpu.VMEM
    rows = vmem((ROWS, D), BF16)
    square = vmem((D, D), BF16)
    padded = vmem((D, PAIRS * LANES), BF16)
    features, stat, grad = pl.pallas_call(
        slide_kernel,
        out_shape=(sds((ROWS, D), BF16), sds((1, 1), F32), sds((D, 256), F32)),
        in_specs=[ANY, VM, ANY, VM, ANY, ANY, ANY, ANY, VM, VM, VM, VM, ANY],
        out_specs=(ANY, pl.BlockSpec(memory_space=pltpu.SMEM), VM),
        scratch_shapes=[
            vmem((ROWS, DIN), BF16), vmem((DIN, D), BF16), square, square, square, square,
            vmem((D, 256), F32), padded, padded, padded, vmem((PAIRS * LANES, D), BF16),
            rows, rows, rows,
            vmem((PEERS, LANES), F32),
            vmem((2 * ROWS, HALF), BF16), vmem((PEERS, 1, LANES), F32),
            vmem((2 * ROWS, HALF), BF16), vmem((PEERS, 1, LANES), F32),
            vmem((8, ROWS), F32), rows, rows,
            vmem((ROWS, 2 * PW), BF16), vmem((2, ROWS, LANES), BF16),
            vmem((DIL, GROUP + 128, PW), BF16), vmem((DIL, GROUP + 128, PW), BF16),
            vmem((DIL, 3 * GROUP, PW), BF16), vmem((DIL, 3 * GROUP, PW), BF16),
            vmem((ROWS, 2 * PW), BF16),
            vmem((2, 8, D), F32), vmem((3, 512, LANES), F32), vmem((3, 512, LANES), F32),
            vmem((512, D), F32),
            dma((8,)), dma, dma, dma, dma, dma((2,)), dma((2, 2, DIL)), dma((2, 2, DIL)),
            dma, dma, dma((3, 19)), dma((3, 19)), pltpu.SemaphoreType.REGULAR,
        ],
        compiler_params=params(collective_id=0, has_side_effects=True),
        name="slide",
    )(
        embeddings, tile_position.reshape(1, ROWS), w_in, ln_gain, w_query, w_key, w_value, w_out,
        near_lengths, far_lengths, tissue.reshape(1, ROWS), hospital.reshape(1, NENC), w_kernel,
    )
    return features, stat.reshape(()), grad


def solution(mesh):
    split = P(("enc", "region"))
    return jax.shard_map(
        local,
        mesh=mesh,
        in_specs=(
            P(("enc", "region"), None), split, P(), P(), P(), P(), P(), P(), P(), P(), split, P(), P(),
        ),
        out_specs=(P(("enc", "region"), None), P(), P()),
        check_vma=False,
    )
```

```python
import functools

import jax
import jax.numpy as jnp
from jax import lax
from jax.experimental import pallas as pl
from jax.experimental.pallas import tpu as pltpu
from jax.sharding import PartitionSpec as P

MESH = pl.DeviceIdType.MESH
F32 = jnp.float32
BF16 = jnp.bfloat16
I32 = jnp.int32

ROWS = 1024
DIN = 1536
D = 768
PAIRS = 8
HEAD = 48
LANES = 128
PW = PAIRS // 2 * LANES
GROUP = 256
DIL = 4
REGION = 256
NENC = 4
NREGION = 32
PEERS = NENC * NREGION
CAP = 8
SEND_UNROLL = 1
SPREAD = 45
HALF = D // 2
EPS = 1e-05
BIG = 1e30
BITS = 9
PAD_SEG = 511
EXP_SCALE = 1.4426950408889634 / 48.0**0.5
VMEM_LIMIT = 60 * 1024 * 1024


def iota(shape, dim):
    return lax.broadcasted_iota(I32, shape, dim)


def dot(a, b):
    return jnp.dot(a, b, preferred_element_type=F32)


def params(**kw):
    return pltpu.CompilerParams(vmem_limit_bytes=VMEM_LIMIT, **kw)


VM = pl.BlockSpec(memory_space=pltpu.VMEM)
ANY = pl.BlockSpec(memory_space=pl.ANY)


def ends_of(lengths):
    n = lengths.shape[1]
    upto = jnp.where(iota((n, n), 0) <= iota((n, n), 1), 1.0, 0.0).astype(BF16)
    high, low = lengths // 32, lengths % 32
    sums = 32.0 * dot(high.astype(F32).astype(BF16), upto) + dot(low.astype(F32).astype(BF16), upto)
    own = iota(sums.shape, 0) == lax.axis_index("enc")
    return jnp.sum(jnp.where(own, sums, 0.0), axis=0, keepdims=True)


def segment_of(pos, ends):
    seg = jnp.sum(jnp.where(ends <= pos.astype(F32), 1.0, 0.0), axis=1, keepdims=True).astype(I32)
    return jnp.where((pos >= 0) & (pos < ROWS * NREGION), seg, PAD_SEG)


def key_marks(seg):
    lane = iota((seg.shape[0], LANES), 1) - 2 * HEAD
    bit = (seg >> jnp.where(lane >= BITS, lane - BITS, jnp.maximum(lane, 0)) % 16) & 1
    mark = jnp.where(lane < BITS, 1 - bit, bit)
    return jnp.where((lane >= 0) & (lane < 2 * BITS), mark, 0).astype(F32)


def query_marks(seg):
    lane = iota((seg.shape[0], LANES), 1) - 2 * HEAD
    bit = (seg >> jnp.where(lane >= BITS, lane - BITS, jnp.maximum(lane, 0)) % 16) & 1
    mark = jnp.where(lane < BITS, bit, 1 - bit)
    return jnp.where((lane >= 0) & (lane < 2 * BITS), mark, 0).astype(F32) * -BIG


def attend(query, marks, key, value):
    n = marks.shape[0]
    lane = iota((n, LANES), 1)
    pairs = range(PAIRS // 2)
    scores = []
    for j in pairs:
        both = query(j)
        q = jnp.concatenate(
            [
                jnp.where((lane >= h * HEAD) & (lane < (h + 1) * HEAD), both, marks)
                for h in range(2)
            ],
            axis=0,
        )
        scores.append(
            lax.dot_general(q, key(j), (((1,), (1,)), ((), ())), preferred_element_type=F32)
        )
    probs = [
        jnp.exp2((s - jnp.max(s, axis=1, keepdims=True)) * EXP_SCALE).astype(BF16) for s in scores
    ]
    out = []
    for j in pairs:
        o = dot(probs[j], value(j))
        o = o / o[:, 2 * HEAD : 2 * HEAD + 1]
        o = jnp.where(lane < HEAD, o[:n], jnp.where(lane < 2 * HEAD, o[n:], 0.0))
        out.append(o.astype(BF16))
    return jnp.concatenate(out, axis=1)


AXES = ("x", "y", "z")


def dot3(a, b, ca=1, cb=0):
    dims = (((ca,), (cb,)), ((), ()))

    def mul(x, y):
        return lax.dot_general(x, y, dims, preferred_element_type=F32)

    ah, bh = a.astype(BF16), b.astype(BF16)
    al, bl = (a - ah.astype(F32)).astype(BF16), (b - bh.astype(F32)).astype(BF16)
    return mul(ah, bh) + (mul(ah, bl) + mul(al, bh))


def slide_kernel(
    emb_hbm, pos_ref, win_hbm, gain_ref, wq_hbm, wk_hbm, wv_hbm, wo_hbm,
    near_ref, far_ref, tissue_ref, hosp_ref, wkern_hbm,
    feat_hbm, stat_ref, grad_ref,
    emb_ref, w_ref, wq_ref, wk_ref, wv_ref, wo_ref, wkern_ref, wq_out, wk_out, wv_out, wo_out,
    start_ref, normed_ref, s_ref, tab_ref, xs_ref, ps_ref, xr_ref, pr_ref,
    sel_ref, left_ref, right_ref, q_ref, qm_ref, kn_ref, vn_ref, kf_ref, vf_ref, ctx_ref,
    pair_ref, half_ref, full_ref, np_ref,
    load_sem, sx, rx, sp, rp, own, send_sem, recv_sem, pair_send, pair_recv, ss, rs, entered,
):
    enc, reg = lax.axis_index("enc"), lax.axis_index("region")
    me = enc * NREGION + reg
    core = reg % 2
    at = {"z": enc, "x": (reg // 2) % 4, "y": reg // 8}

    def device(shift):
        c = {a: (at[a] + shift.get(a, 0)) % 4 for a in AXES}
        return (c["z"], (c["y"] * 4 + c["x"]) * 2 + (core + shift.get("core", 0)) % 2)

    chunk = 2 * CAP
    barrier = pltpu.get_barrier_semaphore()

    plane_yz = [{"z": i, "y": j} for i in range(4) for j in range(4) if i or j]
    line_x = [{"x": i, "core": c} for i in range(4) for c in range(2) if i or c]
    for shift in plane_yz + line_x:
        pl.semaphore_signal(barrier, inc=1, device_id=device(shift), device_id_type=MESH)
    loads = [
        pltpu.make_async_copy(src, dst, load_sem.at[i])
        for i, (src, dst) in enumerate(
            (
                (emb_hbm, emb_ref), (win_hbm, w_ref), (wq_hbm, wq_ref), (wk_hbm, wk_ref),
                (wv_hbm, wv_ref), (wo_hbm, wo_ref), (wkern_hbm, wkern_ref),
            )
        )
    ]
    for c in loads:
        c.start()

    pos = pos_ref[...].astype(F32)
    eye = iota((LANES, LANES), 0) == iota((LANES, LANES), 1)
    rank = jnp.zeros((1, ROWS), F32)
    for k in range(ROWS // LANES):
        part = pos[:, k * LANES : (k + 1) * LANES]
        col = jnp.sum(jnp.where(eye, part, 0.0), axis=1, keepdims=True)
        rank = rank + jnp.sum(jnp.where(col < pos, 1.0, 0.0), axis=0, keepdims=True)
    rank = rank.astype(I32)
    local = pos_ref[...] % ROWS
    slot = ((local % DIL) * GROUP + local // DIL).astype(F32)
    dest = iota((PEERS, ROWS), 0) * CAP
    lane = iota((PEERS, LANES), 1)
    table = jnp.zeros((PEERS, LANES), F32)
    for c in range(CAP):
        hit = jnp.where(dest + c == rank, slot, 0.0)
        table = jnp.where(lane == c, jnp.sum(hit, axis=1, keepdims=True), table)
    tab_ref[...] = table

    def spill(d, carry):
        ps_ref[d] = tab_ref[pl.ds(d, 1), :]
        return carry

    lax.fori_loop(0, PEERS, spill, 0)
    step = 256
    loads[0].wait()
    loads[1].wait()
    for k in range(ROWS // step):
        s_ref[pl.ds(k * step, step), :] = dot(
            emb_ref[pl.ds(k * step, step), :], w_ref[...]
        ).astype(BF16)
    pl.semaphore_wait(barrier, len(plane_yz + line_x))
    for shift in line_x:
        pl.semaphore_signal(entered, inc=1, device_id=device(shift), device_id_type=MESH)
    for k in range(ROWS // step):
        pick = jnp.where(iota((step, ROWS), 0) + k * step == rank, 1.0, 0.0).astype(BF16)
        moved = dot(pick, s_ref[...]).reshape(step // CAP, CAP, D)
        both = jnp.concatenate([moved[:, :, :HALF], moved[:, :, HALF:]], axis=1)
        xs_ref[pl.ds(k * 2 * step, 2 * step), :] = both.reshape(2 * step, HALF).astype(BF16)

    mine_x = pltpu.make_async_copy(
        xs_ref.at[pl.ds(me * chunk, chunk), :], xr_ref.at[pl.ds(me * chunk, chunk), :], own.at[0]
    )
    mine_p = pltpu.make_async_copy(ps_ref.at[me], pr_ref.at[me], own.at[1])
    mine_x.start()
    mine_p.start()
    pl.semaphore_wait(entered, len(line_x))

    def send(k, carry):
        peer = (me + k * SPREAD) % PEERS
        pltpu.make_async_remote_copy(
            src_ref=ps_ref.at[peer], dst_ref=pr_ref.at[me],
            send_sem=sp, recv_sem=rp, device_id=peer, device_id_type=pl.DeviceIdType.LOGICAL,
        ).start()
        pltpu.make_async_remote_copy(
            src_ref=xs_ref.at[pl.ds(peer * chunk, chunk), :],
            dst_ref=xr_ref.at[pl.ds(me * chunk, chunk), :],
            send_sem=sx, recv_sem=rx, device_id=peer, device_id_type=pl.DeviceIdType.LOGICAL,
        ).start()
        return carry

    lax.fori_loop(1, PEERS, send, 0, unroll=SEND_UNROLL)

    for c in loads[2:]:
        c.wait()
    gap = jnp.zeros((D, LANES - 2 * HEAD), BF16)
    for src, dst in ((wq_ref, wq_out), (wk_ref, wk_out), (wv_ref, wv_out)):
        for j in range(PAIRS):
            pair = src[:, 2 * HEAD * j : 2 * HEAD * (j + 1)]
            dst[:, LANES * j : LANES * (j + 1)] = jnp.concatenate([pair, gap], axis=1)
    for j in range(PAIRS):
        wo_out[pl.ds(LANES * j, 2 * HEAD), :] = wo_ref[pl.ds(2 * HEAD * j, 2 * HEAD), :]
        wo_out[pl.ds(LANES * j + 2 * HEAD, LANES - 2 * HEAD), :] = jnp.zeros((LANES - 2 * HEAD, D), BF16)

    chosen = jnp.where(
        iota((8, ROWS), 0) == iota((8, ROWS), 1) // REGION, tissue_ref[...], 0
    ).astype(F32).astype(BF16)
    for o in range(DIL):
        moves = iota((ROWS, GROUP), 0) == iota((ROWS, GROUP), 1) * DIL + o
        sel_ref[:, o * GROUP : (o + 1) * GROUP] = dot(chosen, jnp.where(moves, 1.0, 0.0).astype(BF16))

    mine_x.wait()
    mine_p.wait()
    rest_x = pl.ds(0, (PEERS - 1) * chunk)
    rest_p = pl.ds(0, PEERS - 1)
    pltpu.make_async_copy(ps_ref.at[rest_p], pr_ref.at[rest_p], rp).wait()
    pltpu.make_async_copy(ps_ref.at[rest_p], pr_ref.at[rest_p], sp).wait()

    def fill(d, carry):
        tab_ref[pl.ds(d, 1), :] = pr_ref[d]
        return carry

    lax.fori_loop(0, PEERS, fill, 0)
    table = tab_ref[...]
    high = jnp.floor(table * (1.0 / 32.0))
    low = table - 32.0 * high
    spread = jnp.where(
        iota((LANES, ROWS), 0) == iota((LANES, ROWS), 1) % CAP, 1.0, 0.0
    ).astype(BF16)
    wide = 32.0 * dot(high.astype(BF16), spread) + dot(low.astype(BF16), spread)
    mine = iota((PEERS, ROWS), 0) == iota((PEERS, ROWS), 1) // CAP
    place = jnp.sum(jnp.where(mine, wide, 0.0), axis=0, keepdims=True).astype(I32)

    pltpu.make_async_copy(xs_ref.at[rest_x, :], xr_ref.at[rest_x, :], rx).wait()
    pltpu.make_async_copy(xs_ref.at[rest_x, :], xr_ref.at[rest_x, :], sx).wait()
    for k in range(ROWS // step):
        got = xr_ref[pl.ds(k * 2 * step, 2 * step), :].astype(F32)
        got = got.reshape(step // CAP, 2 * CAP, HALF)
        both = jnp.concatenate([got[:, :CAP, :], got[:, CAP:, :]], axis=2)
        s_ref[pl.ds(k * step, step), :] = both.reshape(step, D).astype(BF16)
    gain = gain_ref[...].astype(F32).reshape(1, D)
    for k in range(ROWS // step):
        pick = jnp.where(iota((step, ROWS), 0) + k * step == place, 1.0, 0.0).astype(BF16)
        rows = dot(pick, s_ref[...])
        start_ref[pl.ds(k * step, step), :] = rows.astype(BF16)
        center = rows - jnp.mean(rows, axis=1, keepdims=True)
        var = jnp.mean(center * center, axis=1, keepdims=True)
        normed_ref[pl.ds(k * step, step), :] = (center * lax.rsqrt(var + EPS) * gain).astype(BF16)

    after, before = (reg + 1) % NREGION, (reg + NREGION - 1) % NREGION
    edge = GROUP // 4
    near_copies, far_copies = [], []
    for kind, copies in ((0, near_copies), (1, far_copies)):
        for o in range(DIL):
            for way, dst, other in ((0, left_ref, after), (1, right_ref, before)):
                first = ((GROUP - edge, 0), (0, edge))[kind][way]
                rows = pl.ds(o * GROUP + first, (edge, GROUP - edge)[kind])
                copies.append(
                    pltpu.make_async_remote_copy(
                        src_ref=normed_ref.at[rows, :], dst_ref=dst.at[rows, :],
                        send_sem=send_sem.at[kind, way, o], recv_sem=recv_sem.at[kind, way, o],
                        device_id=(enc, other), device_id_type=MESH,
                    )
                )
    for c in near_copies:
        c.start()
    for c in far_copies:
        c.start()

    base = reg * ROWS
    near_ends = ends_of(near_ref[...])
    far_ends = ends_of(far_ref[...])
    near_cols, far_cols = pl.ds(0, PW), pl.ds(PW, PW)
    ones_lane = jnp.where(iota((GROUP, PW), 1) % LANES == 2 * HEAD, 1.0, 0.0)

    def tiled(marks):
        return jnp.concatenate([marks] * (PAIRS // 2), axis=1)

    def far_rows(o, b, ref):
        x = ref[pl.ds(o * GROUP, GROUP), :]
        seg = segment_of(base + (b - 1) * ROWS + DIL * iota((GROUP, 1), 0) + o, far_ends)
        dst = pl.ds(b * GROUP, GROUP)
        kf_ref[o, dst, :] = (dot(x, wk_out[:, far_cols]) + tiled(key_marks(seg))).astype(BF16)
        vf_ref[o, dst, :] = (dot(x, wv_out[:, far_cols]) + ones_lane).astype(BF16)
        return seg

    def near_rows(o, b, ref):
        first, count = ((GROUP - edge, edge), (0, GROUP), (0, edge))[b]
        x = ref[pl.ds(o * GROUP + first, count), :]
        pos = base + (b - 1) * ROWS + DIL * (iota((count, 1), 0) + first) + o
        seg = segment_of(pos, near_ends)
        dst = pl.ds((0, edge, edge + GROUP)[b], count)
        kn_ref[o, dst, :] = (dot(x, wk_out[:, near_cols]) + tiled(key_marks(seg))).astype(BF16)
        vn_ref[o, dst, :] = (dot(x, wv_out[:, near_cols]) + ones_lane[:count]).astype(BF16)
        return seg

    for o in range(DIL):
        rows = pl.ds(o * GROUP, GROUP)
        q_ref[rows, :] = dot(normed_ref[rows, :], wq_out[...]).astype(BF16)
        qm_ref[0, rows, :] = query_marks(near_rows(o, 1, normed_ref)).astype(BF16)
        qm_ref[1, rows, :] = query_marks(far_rows(o, 1, normed_ref)).astype(BF16)
    for c in near_copies:
        c.wait()
    for o in range(DIL):
        near_rows(o, 0, left_ref)
        near_rows(o, 2, right_ref)

    def near_block(b, carry):
        g = pl.multiple_of(b * 32, 32)

        def joined(ref, n, j):
            cols = slice(j * LANES, (j + 1) * LANES)
            return jnp.concatenate([ref[o, pl.ds(g, n), cols] for o in range(DIL)], axis=0)

        def query(j):
            cols = slice(j * LANES, (j + 1) * LANES)
            return jnp.concatenate(
                [q_ref[pl.ds(o * GROUP + g, 32), cols] for o in range(DIL)], axis=0
            )

        marks = jnp.concatenate(
            [qm_ref[0, pl.ds(o * GROUP + g, 32), :] for o in range(DIL)], axis=0
        )
        out = attend(query, marks, lambda j: joined(kn_ref, 160, j), lambda j: joined(vn_ref, 160, j))
        for o in range(DIL):
            ctx_ref[pl.ds(o * GROUP + g, 32), near_cols] = out[o * 32 : (o + 1) * 32, :]
        return carry

    lax.fori_loop(0, ROWS // 128, near_block, 0)
    for o in range(DIL):
        for c in far_copies[2 * o : 2 * o + 2]:
            c.wait()
        far_rows(o, 0, left_ref)
        far_rows(o, 2, right_ref)

    def far_block(i, carry):
        o, half = i // 2, i % 2
        g = pl.multiple_of(half * 128, 128)
        rows = pl.ds(pl.multiple_of(o * GROUP + g, 128), 128)
        ctx_ref[rows, far_cols] = attend(
            lambda j: q_ref[rows, PW + j * LANES : PW + (j + 1) * LANES],
            qm_ref[1, rows, :],
            lambda j: kf_ref[o, pl.ds(g, 640), j * LANES : (j + 1) * LANES],
            lambda j: vf_ref[o, pl.ds(g, 640), j * LANES : (j + 1) * LANES],
        )
        return carry

    lax.fori_loop(0, ROWS // 128, far_block, 0)

    for o in range(DIL):
        rows = pl.ds(o * GROUP, GROUP)
        out = start_ref[rows, :].astype(F32) + dot(ctx_ref[rows, :], wo_out[...])
        s_ref[rows, :] = out.astype(BF16)
    pooled = dot(sel_ref[...].astype(BF16), s_ref[...]) / REGION

    def reorder(k):
        r = iota((step, ROWS), 0) + k * step
        pick = jnp.where(
            iota((step, ROWS), 1) == (r % DIL) * GROUP + r // DIL, 1.0, 0.0
        ).astype(BF16)
        normed_ref[pl.ds(k * step, step), :] = dot(pick, s_ref[...]).astype(BF16)

    center = pooled - jnp.mean(pooled, axis=1, keepdims=True)
    var = jnp.mean(center * center, axis=1, keepdims=True)
    norm = center * lax.rsqrt(var + EPS)
    row = iota((8, D), 0)
    norm = jnp.where(row < 4, norm, 0.0)
    swapped = jnp.concatenate([norm[4:], norm[:4]], axis=0)
    pair_ref[0] = jnp.where(core == 0, norm, swapped)
    first = pltpu.make_async_remote_copy(
        src_ref=pair_ref.at[0], dst_ref=pair_ref.at[1], send_sem=pair_send, recv_sem=pair_recv,
        device_id=device({"core": 1}), device_id_type=MESH,
    )
    first.start()
    reorder(0)
    first.wait()
    chip = pair_ref[0] + pair_ref[1]
    mine = jnp.where(core == 0, chip[:, :HALF], chip[:, HALF:])
    orders = [("z", "y", "x"), ("y", "x", "z"), ("x", "z", "y")]

    def offset(order):
        return ((at[order[2]] * 4 + at[order[1]]) * 4 + at[order[0]]) * 8

    for t, order in enumerate(orders):
        start = pl.multiple_of(offset(order), 8)
        half_ref[t, pl.ds(start, 8), :] = mine[:, t * LANES : (t + 1) * LANES]
    def plane(order):
        return [{order[0]: a, order[1]: b} for a in range(4) for b in range(4) if a or b]

    def remote(window, sems, peer):
        return pltpu.make_async_remote_copy(
            src_ref=window, dst_ref=window, send_sem=ss.at[sems], recv_sem=rs.at[sems],
            device_id=device(peer), device_id_type=MESH,
        )

    first, second, third = [], [], []
    for t, order in enumerate(orders):
        start = pl.multiple_of(offset(order), 8)
        window = half_ref.at[t, pl.ds(start, 8), :]
        first.append([remote(window, (t, i), p) for i, p in enumerate(plane(order))])
        window = half_ref.at[t, pl.ds(pl.multiple_of(start // 128 * 128, 128), 128), :]
        second.append([remote(window, (t, 15 + k), {order[2]: k + 1}) for k in range(3)])
        third.append(
            pltpu.make_async_remote_copy(
                src_ref=half_ref.at[t], dst_ref=full_ref.at[t],
                send_sem=ss.at[t, 18], recv_sem=rs.at[t, 18],
                device_id=device({"core": 1}), device_id_type=MESH,
            )
        )
    for copies in first:
        for c in copies:
            c.start()
    for k in range(1, ROWS // step):
        reorder(k)
    store = pltpu.make_async_copy(normed_ref, feat_hbm, load_sem.at[7])
    store.start()
    for t in range(3):
        for c in first[t]:
            c.wait()
        for c in second[t]:
            c.start()
    for t in range(3):
        for c in second[t]:
            c.wait()
        third[t].start()
    for t in range(3):
        third[t].wait()

    for x in range(4):
        for y in range(4):
            for z in range(4):
                i = {"x": x, "y": y, "z": z}
                to = pl.ds(((x * 4 + y) * 4 + z) * 8, 8)
                for t, order in enumerate(orders):
                    src = pl.ds(((i[order[2]] * 4 + i[order[1]]) * 4 + i[order[0]]) * 8, 8)
                    a, b = half_ref[t, src, :], full_ref[t, src, :]
                    np_ref[to, t * LANES : (t + 1) * LANES] = jnp.where(core == 0, a, b)
                    np_ref[to, HALF + t * LANES : HALF + (t + 1) * LANES] = jnp.where(core == 0, b, a)

    n = PEERS * 4
    hp = lax.Precision.HIGHEST
    hosp = hosp_ref[...]
    ones = jnp.sum(hosp).astype(F32)
    per_slide = float(n // NENC)
    count_one = ones * per_slide
    count_zero = (NENC - ones) * per_slide

    def weights(slide, axis):
        label = jnp.zeros(slide.shape, I32)
        for s in range(NENC):
            label = jnp.where(slide == s, hosp[:, s : s + 1], label)
        return jnp.where(label == 1, 1.0 / count_one, -1.0 / count_zero)

    w_col = weights((iota((n, 1), 0) // 8) % 4, 0)
    w_row = weights((iota((1, n), 1) // 8) % 4, 1)
    normal = np_ref[...]
    emb = dot3(normal, wkern_ref[...])
    sq = emb * emb
    sq_col = jnp.sum(sq, axis=1, keepdims=True)
    sq_row = lax.dot_general(
        jnp.ones((8, sq.shape[1]), F32), sq, (((1,), (1,)), ((), ())), precision=hp,
        preferred_element_type=F32,
    )[0:1, :]
    inner = dot3(emb, emb, 1, 1)
    kern = jnp.exp(-(sq_col + sq_row - 2.0 * inner) / (2.0 * emb.shape[1])) * w_row
    sums = jnp.sum(kern, axis=1, keepdims=True)
    moments = dot3(kern, emb)
    stat = n * jnp.sum(w_col * sums)
    stat_ref[0, 0] = stat
    g = (-2.0 * n / emb.shape[1]) * w_col * (sums * emb - moments)
    grad_ref[...] = 100.0 * dot3(normal, g, 0, 0)
    store.wait()


def local(
    embeddings, tile_position, w_in, ln_gain, w_query, w_key, w_value, w_out,
    near_lengths, far_lengths, tissue, hospital, w_kernel,
):
    sds = jax.ShapeDtypeStruct
    dma, vmem = pltpu.SemaphoreType.DMA, pltpu.VMEM
    rows = vmem((ROWS, D), BF16)
    square = vmem((D, D), BF16)
    padded = vmem((D, PAIRS * LANES), BF16)
    features, stat, grad = pl.pallas_call(
        slide_kernel,
        out_shape=(sds((ROWS, D), BF16), sds((1, 1), F32), sds((D, 256), F32)),
        in_specs=[ANY, VM, ANY, VM, ANY, ANY, ANY, ANY, VM, VM, VM, VM, ANY],
        out_specs=(ANY, pl.BlockSpec(memory_space=pltpu.SMEM), VM),
        scratch_shapes=[
            vmem((ROWS, DIN), BF16), vmem((DIN, D), BF16), square, square, square, square,
            vmem((D, 256), F32), padded, padded, padded, vmem((PAIRS * LANES, D), BF16),
            rows, rows, rows,
            vmem((PEERS, LANES), F32),
            vmem((2 * ROWS, HALF), BF16), vmem((PEERS, 1, LANES), F32),
            vmem((2 * ROWS, HALF), BF16), vmem((PEERS, 1, LANES), F32),
            vmem((8, ROWS), F32), rows, rows,
            vmem((ROWS, 2 * PW), BF16), vmem((2, ROWS, LANES), BF16),
            vmem((DIL, GROUP + 128, PW), BF16), vmem((DIL, GROUP + 128, PW), BF16),
            vmem((DIL, 3 * GROUP, PW), BF16), vmem((DIL, 3 * GROUP, PW), BF16),
            vmem((ROWS, 2 * PW), BF16),
            vmem((2, 8, D), F32), vmem((3, 512, LANES), F32), vmem((3, 512, LANES), F32),
            vmem((512, D), F32),
            dma((8,)), dma, dma, dma, dma, dma((2,)), dma((2, 2, DIL)), dma((2, 2, DIL)),
            dma, dma, dma((3, 19)), dma((3, 19)), pltpu.SemaphoreType.REGULAR,
        ],
        compiler_params=params(collective_id=0, has_side_effects=True),
        name="slide",
    )(
        embeddings, tile_position.reshape(1, ROWS), w_in, ln_gain, w_query, w_key, w_value, w_out,
        near_lengths, far_lengths, tissue.reshape(1, ROWS), hospital.reshape(1, NENC), w_kernel,
    )
    return features, stat.reshape(()), grad


def solution(mesh):
    split = P(("enc", "region"))
    return jax.shard_map(
        local,
        mesh=mesh,
        in_specs=(
            P(("enc", "region"), None), split, P(), P(), P(), P(), P(), P(), P(), P(), split, P(), P(),
        ),
        out_specs=(P(("enc", "region"), None), P(), P()),
        check_vma=False,
    )
```
